32 devices in a mesh: dp: 4 (over y, x), mp: 8 (over z, core).
Axes of the slice: x: 2, y: 2, z: 4, core: 2. Of those that a mesh axis runs over, the one named last changes fastest.
Arguments:
- queries: bfloat16 [3, 2048, 4096], P(None, 'dp', 'mp'), may hold values from -15 to 15
- memory: bfloat16 [128, 4096], P('mp'), may hold values from -6 to 6
- w_key: bfloat16 [3, 4096, 4096], P(None, 'mp'), may hold values from -0.09375 to 0.09375
- w_value: bfloat16 [3, 4096, 4096], P(None, 'mp'), may hold values from -0.09375 to 0.09375
- grad_out: bfloat16 [3, 2048, 4096], P(None, 'dp', 'mp'), may hold values from -6 to 6
Outputs:
- attended: bfloat16 [3, 2048, 4096], P(None, 'dp', 'mp')
- grad_queries: bfloat16 [3, 2048, 4096], P(None, 'dp', 'mp')
- grad_memory: float32 [128, 4096], P('mp')
- grad_w_key: float32 [3, 4096, 4096], P(None, 'mp')
- grad_w_value: float32 [3, 4096, 4096], P(None, 'mp')
The draws below stay inside these ranges and needn't reach their ends.
All inputs are finite; a program needn't handle non-finite values.
Results may differ from the reference program's by a relative error of at most 0.025.
Values may be sent and summed in bfloat16 or wider, within the bound.
A program may use at most 128 MiB of HBM per device.

```python
import jax
import jax.numpy as jnp
from jax import lax

D = 4096
HEAD_COUNT = 64
HEAD_WIDTH = 64
LAYERS = 3
E = 4096
ENCODER_TOKENS = 128
DECODER_TOKENS = 2048


def draw_queries(key, part):
    key = jax.random.fold_in(key, 7)
    base = jax.random.truncated_normal(key, -4.0, 4.0, (LAYERS, DECODER_TOKENS, HEAD_COUNT * HEAD_WIDTH), jnp.float32) * 0.375
    return base.astype(jnp.bfloat16)


def level_of(own_key, shape, shards, smallest, largest):
    factor_of, own = 1.0, jax.random.fold_in(own_key, 6)
    for axis_at, blocks in shards:
        steps = jnp.exp(jax.random.uniform(jax.random.fold_in(own, axis_at), (blocks,), jnp.float32, smallest / len(shards), largest / len(shards)))
        factor_of = factor_of * jnp.repeat(steps, shape[axis_at] // blocks).reshape([-1 if axis == axis_at else 1 for axis in range(len(shape))])
    return factor_of


def noise(stream_key, extent, width, limit, cuts=(), held_as=jnp.bfloat16):
    result = jax.random.normal(stream_key, extent, jnp.float32) * width
    if len(cuts) > 0:
        result = level_of(stream_key, extent, cuts, -0.22, 0.18) * result
    return jnp.clip(result, min=-limit, max=limit).astype(held_as)


def setup_inputs(seed: int = 0) -> dict:
    key_of = jax.random.split(jax.random.key(seed), 6)
    return {
        "queries": draw_queries(jax.random.fold_in(key_of[5], 71), 0),
        "memory": noise(key_of[1], (ENCODER_TOKENS, D), 1.0, 6.0, ((0, 8),)),
        "w_key": noise(key_of[2], (LAYERS, E, D), D ** -0.5, 0.09375, ((1, 8),)),
        "w_value": noise(key_of[3], (LAYERS, E, D), D ** -0.5, 0.09375, ((1, 8),)),
        "grad_out": noise(key_of[4], (LAYERS, DECODER_TOKENS, E), 1.0, 6.0, ((1, 4), (2, 8))),
    }


def reference(queries, memory, w_key, w_value, grad_out):
    attended = []
    grad_queries = []
    grad_w_key = []
    grad_w_value = []
    grad_memory = jnp.zeros((ENCODER_TOKENS, memory.shape[1]), jnp.float32)
    for layer in range(LAYERS):
        keys = jnp.dot(memory, w_key[layer].T, preferred_element_type=jnp.float32).astype(jnp.bfloat16)
        values = jnp.dot(memory, w_value[layer].T, preferred_element_type=jnp.float32).astype(jnp.bfloat16)
        per_head_queries = queries[layer].reshape(DECODER_TOKENS, HEAD_COUNT, HEAD_WIDTH).astype(jnp.float32)
        per_head_keys = keys.reshape(ENCODER_TOKENS, HEAD_COUNT, HEAD_WIDTH).astype(jnp.float32)
        per_head_values = values.reshape(ENCODER_TOKENS, HEAD_COUNT, HEAD_WIDTH).astype(jnp.float32)
        head_output_gradient = grad_out[layer].reshape(DECODER_TOKENS, HEAD_COUNT, HEAD_WIDTH).astype(jnp.float32)
        attention_logits = jnp.einsum('fke,pke->kfp', per_head_queries, per_head_keys)
        row_max = jnp.max(attention_logits, axis=-1, keepdims=True)
        exp_scores = jnp.exp(attention_logits - row_max)
        attn_probs = exp_scores / jnp.sum(exp_scores, axis=-1, keepdims=True)
        batch_probabilities = lax.optimization_barrier(attn_probs.astype(jnp.bfloat16)).astype(jnp.float32)
        attended_output = jnp.einsum('kqc,cke->qke', batch_probabilities, per_head_values).reshape(DECODER_TOKENS, HEAD_COUNT * HEAD_WIDTH)
        attended.append(attended_output.astype(jnp.bfloat16))
        probability_gradient = jnp.einsum('fke,pke->kfp', head_output_gradient, per_head_values)
        row_delta = jnp.sum(attn_probs * probability_gradient, axis=-1, keepdims=True)
        logit_gradient = lax.optimization_barrier((attn_probs * (probability_gradient - row_delta)).astype(jnp.bfloat16)).astype(jnp.float32)
        query_gradient = jnp.einsum('kqc,cke->qke', logit_gradient, per_head_keys).reshape(DECODER_TOKENS, HEAD_COUNT * HEAD_WIDTH)
        grad_queries.append(query_gradient.astype(jnp.bfloat16))
        key_gradient = jnp.einsum('vlk,lvu->kvu', logit_gradient, per_head_queries).reshape(ENCODER_TOKENS, HEAD_COUNT * HEAD_WIDTH).astype(jnp.bfloat16)
        value_gradient = jnp.einsum('vlk,lvu->kvu', batch_probabilities, head_output_gradient).reshape(ENCODER_TOKENS, HEAD_COUNT * HEAD_WIDTH).astype(jnp.bfloat16)
        grad_w_key.append(jnp.dot(key_gradient.T, memory, preferred_element_type=jnp.float32))
        grad_w_value.append(jnp.dot(value_gradient.T, memory, preferred_element_type=jnp.float32))
        grad_memory = grad_memory + jnp.dot(key_gradient, w_key[layer], preferred_element_type=jnp.float32)
        grad_memory = grad_memory + jnp.dot(value_gradient, w_value[layer], preferred_element_type=jnp.float32)
    return (jnp.stack(attended), jnp.stack(grad_queries), grad_memory, jnp.stack(grad_w_key), jnp.stack(grad_w_value))
```

```python
import jax
import jax.numpy as jnp
from jax import lax
from jax.experimental import pallas as pl
from jax.experimental.pallas import tpu as pltpu
from jax.sharding import PartitionSpec as P

HEAD_WIDTH = 64
PAIR = 2 * HEAD_WIDTH
MESH = pl.DeviceIdType.MESH
F32 = jnp.float32
BF16 = jnp.bfloat16

DP, CHIPS, CORES = 4, 4, 2


def attention_kernel(
    q_hbm, mem_ref, wk_hbm, wv_hbm, g_hbm,
    att_hbm, gq_hbm, kvg_hbm, mem_hbm, gm_hbm,
    q_v, g_v, att_v, gq_v, w_v, mg, acc, kvt, part, own, landed, kvg, gm_v,
    in_sem, w_sem, out_sem, z_send, z_recv, d_send, d_recv, s_send, s_recv,
    rs_send, rs_recv, ag_send, ag_recv,
):
    layers, rows, width = q_v.shape
    tokens = mem_ref.shape[0]
    quarter = mem_ref.shape[1] // DP
    mem_total = tokens * CHIPS * CORES
    i = lax.axis_index("dp")
    me = lax.axis_index("mp")
    z = me // CORES
    core = me % CORES
    sibling = z * CORES + 1 - core

    def z_peer(k):
        return {"dp": i, "mp": ((z + k) % CHIPS) * CORES + core}

    def d_peer(k):
        return {"dp": (i + k) % DP, "mp": me}

    sib = {"dp": i, "mp": sibling}

    def load_w(step):
        j = (i + DP - step) % DP
        cols = pl.ds(pl.multiple_of(j * quarter, quarter), quarter)
        return [
            pltpu.make_async_copy(
                hbm.at[:, :, cols], w_v.at[:, kv, :, cols], w_sem.at[step, kv]
            )
            for kv, hbm in enumerate((wk_hbm, wv_hbm))
        ]

    for step in range(DP):
        for copy in load_w(step):
            copy.start()
        if step == 0:
            load_q = pltpu.make_async_copy(q_hbm, q_v, in_sem.at[0])
            load_g = pltpu.make_async_copy(g_hbm, g_v, in_sem.at[1])
    load_q.start()
    load_g.start()

    barrier = pltpu.get_barrier_semaphore()
    for k in range(1, CHIPS):
        pl.semaphore_signal(barrier, inc=1, device_id=z_peer(k), device_id_type=MESH)
    for k in range(1, DP):
        pl.semaphore_signal(barrier, inc=1, device_id=d_peer(k), device_id_type=MESH)
    pl.semaphore_signal(barrier, inc=1, device_id=sib, device_id_type=MESH)
    pl.semaphore_wait(barrier, CHIPS + DP - 1)

    mine = pl.ds(pl.multiple_of(i * quarter, quarter), quarter)
    z_copies = []
    for k in range(1, CHIPS):
        z_copies.append(
            pltpu.make_async_remote_copy(
                src_ref=mem_ref.at[:, mine],
                dst_ref=mg.at[i, core, z],
                send_sem=z_send.at[k - 1],
                recv_sem=z_recv.at[k - 1],
                device_id=z_peer(k),
                device_id_type=MESH,
            )
        )
        z_copies[-1].start()
    mg[i, core, z] = mem_ref[:, mine]
    for copy in z_copies:
        copy.wait_recv()

    def to_sibling(step):
        j = (i + DP - step) % DP
        return pltpu.make_async_remote_copy(
            src_ref=mg.at[j, core],
            dst_ref=mg.at[j, core],
            send_sem=s_send.at[step],
            recv_sem=s_recv.at[step],
            device_id=sib,
            device_id_type=MESH,
        )

    d_copies = []
    s_copies = [to_sibling(0)]
    s_copies[0].start()
    for k in range(1, DP):
        d_copies.append(
            pltpu.make_async_remote_copy(
                src_ref=mg.at[i, core],
                dst_ref=mg.at[i, core],
                send_sem=d_send.at[k - 1],
                recv_sem=d_recv.at[k - 1],
                device_id=d_peer(k),
                device_id_type=MESH,
            )
        )
        d_copies[-1].start()

    acc[...] = jnp.zeros_like(acc)
    for step in range(DP):
        j = (i + DP - step) % DP
        cols = pl.ds(pl.multiple_of(j * quarter, quarter), quarter)
        if step >= 1:
            d_copies[step - 1].wait_recv()
            s_copies.append(to_sibling(step))
            s_copies[step].start()
        for copy in load_w(step):
            copy.wait()
        s_copies[step].wait_recv()

        @pl.loop(0, layers * 2)
        def project(n):
            mem_cols = mg[j].reshape(mem_total, quarter)
            acc[n // 2, n % 2] += lax.dot_general(
                w_v[n // 2, n % 2, :, cols],
                mem_cols,
                (((1,), (1,)), ((), ())),
                preferred_element_type=F32,
            )

    kvt[...] = acc[...].astype(BF16)
    for copy in z_copies + d_copies + s_copies:
        copy.wait_send()
    mem_out = pltpu.make_async_copy(mg, mem_hbm, out_sem.at[0])
    mem_out.start()
    load_q.wait()
    load_g.wait()

    def pair_rows(pair):
        return pl.ds(pl.multiple_of(pair * PAIR, PAIR), PAIR)

    def rs_copy(layer, t):
        return pltpu.make_async_remote_copy(
            src_ref=part.at[layer, t],
            dst_ref=landed.at[layer, t],
            send_sem=rs_send.at[layer, t],
            recv_sem=rs_recv.at[layer, t],
            device_id={"dp": (i + 1 + t) % DP, "mp": me},
            device_id_type=MESH,
        )

    def ag_copy(layer, k):
        block = kvg.at[layer, :, pair_rows(i), :]
        return pltpu.make_async_remote_copy(
            src_ref=block,
            dst_ref=block,
            send_sem=ag_send.at[layer, k - 1],
            recv_sem=ag_recv.at[layer, k - 1],
            device_id=d_peer(k),
            device_id_type=MESH,
        )

    def reduce(layer):
        total = own[layer]
        for t in range(DP - 1):
            rs_copy(layer, t).wait_recv()
            total = total + landed[layer, t].astype(F32)
        kvg[layer, :, pair_rows(i), :] = total.astype(BF16)
        for k in range(1, DP):
            ag_copy(layer, k).start()

    first_head = lax.broadcasted_iota(jnp.int32, (PAIR, mem_total), 0) < HEAD_WIDTH

    def block_diagonal(block):
        zero = jnp.zeros_like(block)
        return jnp.concatenate(
            [jnp.where(first_head, block, zero), jnp.where(first_head, zero, block)], axis=1
        )

    def own_blocks(both):
        return jnp.where(first_head, both[:, :mem_total], both[:, mem_total:])

    @pl.loop(0, layers * DP)
    def attend(n):
        layer = n // DP
        t = n % DP
        pair = (i + 1 + t) % DP
        lanes = pair_rows(pair)
        queries = q_v[layer, :, lanes]
        grads = g_v[layer, :, lanes]
        keys = block_diagonal(kvt[layer, 0, lanes, :])
        values = block_diagonal(kvt[layer, 1, lanes, :])
        scores = jnp.dot(queries, keys, preferred_element_type=F32)
        grad_probs = jnp.dot(grads, values, preferred_element_type=F32)
        probs_b, grad_scores = [], []
        for head in range(2):
            at = slice(head * mem_total, (head + 1) * mem_total)
            s = scores[:, at]
            gp = grad_probs[:, at]
            e = jnp.exp(s - jnp.max(s, axis=-1, keepdims=True))
            probs = e * (1.0 / jnp.sum(e, axis=-1, keepdims=True))
            delta = jnp.sum(probs * gp, axis=-1, keepdims=True)
            probs_b.append(probs.astype(BF16))
            grad_scores.append((probs * (gp - delta)).astype(BF16))
        probs_b = jnp.concatenate(probs_b, axis=1)
        grad_scores = jnp.concatenate(grad_scores, axis=1)
        nt = (((1,), (1,)), ((), ()))
        tn = (((0,), (0,)), ((), ()))
        att_v[layer, :, lanes] = lax.dot_general(
            probs_b, values, nt, preferred_element_type=F32
        ).astype(BF16)
        gq_v[layer, :, lanes] = lax.dot_general(
            grad_scores, keys, nt, preferred_element_type=F32
        ).astype(BF16)
        grad_keys = own_blocks(
            lax.dot_general(queries, grad_scores, tn, preferred_element_type=F32)
        )
        grad_values = own_blocks(
            lax.dot_general(grads, probs_b, tn, preferred_element_type=F32)
        )

        @pl.when(t < DP - 1)
        def _():
            part[layer, t, 0] = grad_keys.astype(BF16)
            part[layer, t, 1] = grad_values.astype(BF16)
            rs_copy(layer, t).start()

        @pl.when(t == DP - 1)
        def _():
            own[layer, 0] = grad_keys
            own[layer, 1] = grad_values

        @pl.when((t == 1) & (layer >= 1))
        def _():
            reduce(layer - 1)

    att_out = pltpu.make_async_copy(att_v, att_hbm, out_sem.at[1])
    gq_out = pltpu.make_async_copy(gq_v, gq_hbm, out_sem.at[2])
    att_out.start()
    gq_out.start()
    reduce(layers - 1)

    for layer in range(layers):
        for k in range(1, DP):
            ag_copy(layer, k).wait_recv()
        for kv in range(2):
            term = lax.dot_general(
                kvg[layer, kv],
                w_v[layer, kv, :, mine],
                (((0,), (0,)), ((), ())),
                preferred_element_type=F32,
            )
            if layer == 0 and kv == 0:
                gm_v[...] = term
            else:
                gm_v[...] += term
    for layer in range(layers):
        for t in range(DP - 1):
            rs_copy(layer, t).wait_send()
            ag_copy(layer, t + 1).wait_send()
    kvg_out = pltpu.make_async_copy(kvg, kvg_hbm, out_sem.at[3])
    gm_out = pltpu.make_async_copy(gm_v, gm_hbm, out_sem.at[4])
    kvg_out.start()
    gm_out.start()
    for copy in (mem_out, att_out, gq_out, kvg_out, gm_out):
        copy.wait()


def attention(queries, memory, w_key, w_value, grad_out):
    layers, rows, width = queries.shape
    tokens, model = memory.shape
    quarter = model // DP
    mem_total = tokens * CHIPS * CORES
    any_spec = pl.BlockSpec(memory_space=pl.ANY)
    dma = pltpu.SemaphoreType.DMA
    out_shape = (
        jax.ShapeDtypeStruct(queries.shape, BF16),
        jax.ShapeDtypeStruct(queries.shape, BF16),
        jax.ShapeDtypeStruct((layers, 2, width, mem_total), BF16),
        jax.ShapeDtypeStruct((DP, CORES, CHIPS, tokens, quarter), BF16),
        jax.ShapeDtypeStruct((mem_total, quarter), F32),
    )
    return pl.pallas_call(
        attention_kernel,
        out_shape=out_shape,
        in_specs=[
            any_spec,
            pl.BlockSpec(memory_space=pltpu.VMEM),
            any_spec,
            any_spec,
            any_spec,
        ],
        out_specs=(any_spec,) * 5,
        scratch_shapes=[
            pltpu.VMEM(queries.shape, BF16),
            pltpu.VMEM(queries.shape, BF16),
            pltpu.VMEM(queries.shape, BF16),
            pltpu.VMEM(queries.shape, BF16),
            pltpu.VMEM((layers, 2, width, model), BF16),
            pltpu.VMEM((DP, CORES, CHIPS, tokens, quarter), BF16),
            pltpu.VMEM((layers, 2, width, mem_total), F32),
            pltpu.VMEM((layers, 2, width, mem_total), BF16),
            pltpu.VMEM((layers, DP - 1, 2, PAIR, mem_total), BF16),
            pltpu.VMEM((layers, 2, PAIR, mem_total), F32),
            pltpu.VMEM((layers, DP - 1, 2, PAIR, mem_total), BF16),
            pltpu.VMEM((layers, 2, width, mem_total), BF16),
            pltpu.VMEM((mem_total, quarter), F32),
            dma((2,)),
            dma((DP, 2)),
            dma((5,)),
            dma((CHIPS - 1,)),
            dma((CHIPS - 1,)),
            dma((DP - 1,)),
            dma((DP - 1,)),
            dma((DP,)),
            dma((DP,)),
            dma((layers, DP - 1)),
            dma((layers, DP - 1)),
            dma((layers, DP - 1)),
            dma((layers, DP - 1)),
        ],
        compiler_params=pltpu.CompilerParams(
            collective_id=0, has_side_effects=True, vmem_limit_bytes=52 * 2**20
        ),
        cost_estimate=pl.CostEstimate(
            flops=8 * 10**9, bytes_accessed=35 * 10**6, transcendentals=2 * 10**6
        ),
        name="attention",
    )(queries, memory, w_key, w_value, grad_out)


def weight_kernel(kvg_ref, mem_ref, gwk_ref, gwv_ref):
    quarter = mem_ref.shape[-1]
    for kv, out in enumerate((gwk_ref, gwv_ref)):
        for j in range(DP):
            out[0, :, j * quarter : (j + 1) * quarter] = jnp.dot(
                kvg_ref[0, kv], mem_ref[j], preferred_element_type=F32
            )


def weight_gradients(kvg, mem):
    layers, _, width, mem_total = kvg.shape
    quarter = mem.shape[-1]
    model = DP * quarter
    rows = 128
    out = jax.ShapeDtypeStruct((layers, width, model), F32)
    return pl.pallas_call(
        weight_kernel,
        grid=(layers, width // rows),
        in_specs=[
            pl.BlockSpec((1, 2, rows, mem_total), lambda l, c: (l, 0, c, 0)),
            pl.BlockSpec((DP, mem_total, quarter), lambda l, c: (0, 0, 0)),
        ],
        out_specs=[pl.BlockSpec((1, rows, model), lambda l, c: (l, c, 0))] * 2,
        out_shape=(out, out),
        compiler_params=pltpu.CompilerParams(vmem_limit_bytes=32 * 2**20),
        cost_estimate=pl.CostEstimate(
            flops=4 * layers * width * mem_total * model,
            bytes_accessed=8 * layers * width * model,
            transcendentals=0,
        ),
        name="weight_gradients",
    )(kvg, mem)


def fused_shards(queries, memory, w_key, w_value, grad_out):
    attended, grad_queries, kvg, mem, gm_part = attention(
        queries, memory, w_key, w_value, grad_out
    )
    tokens = memory.shape[0]
    mem_total = tokens * CHIPS * CORES
    quarter = mem.shape[-1]
    gm_part = (
        gm_part.reshape(CORES, CHIPS, tokens, quarter)
        .transpose(1, 0, 2, 3)
        .reshape(mem_total, quarter)
    )
    gm = lax.psum_scatter(gm_part, "mp", scatter_dimension=0, tiled=True)
    grad_memory = lax.all_gather(gm, "dp", axis=1, tiled=True)
    grad_w_key, grad_w_value = weight_gradients(kvg, mem.reshape(DP, mem_total, quarter))
    return attended, grad_queries, grad_memory, grad_w_key, grad_w_value


def shards(queries, memory, w_key, w_value, grad_out):
    layers, rows, width = queries.shape
    heads_dev = width // HEAD_WIDTH
    mem_all = lax.all_gather(memory, "mp", axis=0, tiled=True)
    mem_total = mem_all.shape[0]
    keys = jnp.einsum("md,lcd->lmc", mem_all, w_key, preferred_element_type=jnp.float32).astype(
        jnp.bfloat16
    )
    values = jnp.einsum("md,lcd->lmc", mem_all, w_value, preferred_element_type=jnp.float32).astype(
        jnp.bfloat16
    )
    per_head_queries = queries.reshape(layers, rows, heads_dev, HEAD_WIDTH)
    per_head_keys = keys.reshape(layers, mem_total, heads_dev, HEAD_WIDTH)
    per_head_values = values.reshape(layers, mem_total, heads_dev, HEAD_WIDTH)
    head_output_gradient = grad_out.reshape(layers, rows, heads_dev, HEAD_WIDTH)
    attention_logits = jnp.einsum(
        "lrhd,lmhd->lhrm", per_head_queries, per_head_keys, preferred_element_type=jnp.float32
    )
    row_max = jnp.max(attention_logits, axis=-1, keepdims=True)
    exp_scores = jnp.exp(attention_logits - row_max)
    attn_probs = exp_scores / jnp.sum(exp_scores, axis=-1, keepdims=True)
    batch_probabilities = attn_probs.astype(jnp.bfloat16)
    attended = (
        jnp.einsum(
            "lhrm,lmhd->lrhd",
            batch_probabilities,
            per_head_values,
            preferred_element_type=jnp.float32,
        )
        .reshape(layers, rows, width)
        .astype(jnp.bfloat16)
    )
    probability_gradient = jnp.einsum(
        "lrhd,lmhd->lhrm", head_output_gradient, per_head_values, preferred_element_type=jnp.float32
    )
    row_delta = jnp.sum(attn_probs * probability_gradient, axis=-1, keepdims=True)
    logit_gradient = (attn_probs * (probability_gradient - row_delta)).astype(jnp.bfloat16)
    grad_queries = (
        jnp.einsum(
            "lhrm,lmhd->lrhd", logit_gradient, per_head_keys, preferred_element_type=jnp.float32
        )
        .reshape(layers, rows, width)
        .astype(jnp.bfloat16)
    )
    key_part = jnp.einsum(
        "lhrm,lrhd->lmhd", logit_gradient, per_head_queries, preferred_element_type=jnp.float32
    ).reshape(layers, mem_total, width)
    value_part = jnp.einsum(
        "lhrm,lrhd->lmhd",
        batch_probabilities,
        head_output_gradient,
        preferred_element_type=jnp.float32,
    ).reshape(layers, mem_total, width)
    key_sum, value_sum = lax.psum((key_part, value_part), "dp")
    key_gradient = key_sum.astype(jnp.bfloat16)
    value_gradient = value_sum.astype(jnp.bfloat16)
    grad_w_key = jnp.einsum(
        "lmc,md->lcd", key_gradient, mem_all, preferred_element_type=jnp.float32
    )
    grad_w_value = jnp.einsum(
        "lmc,md->lcd", value_gradient, mem_all, preferred_element_type=jnp.float32
    )
    grad_memory = lax.psum_scatter(
        jnp.einsum("lmc,lcd->md", key_gradient, w_key, preferred_element_type=jnp.float32)
        + jnp.einsum("lmc,lcd->md", value_gradient, w_value, preferred_element_type=jnp.float32),
        "mp",
        scatter_dimension=0,
        tiled=True,
    )
    return (attended, grad_queries, grad_memory, grad_w_key, grad_w_value)


def solution(mesh):
    def choose(queries, memory, w_key, w_value, grad_out):
        fits = (
            mesh.shape["dp"] == DP
            and mesh.shape["mp"] == CHIPS * CORES
            and queries.shape[2] == DP * PAIR
            and memory.shape[0] == 16
            and memory.shape[1] % (DP * 128) == 0
        )
        run = fused_shards if fits else shards
        return run(queries, memory, w_key, w_value, grad_out)

    return jax.shard_map(
        choose,
        mesh=mesh,
        in_specs=(
            P(None, "dp", "mp"),
            P("mp", None),
            P(None, "mp", None),
            P(None, "mp", None),
            P(None, "dp", "mp"),
        ),
        out_specs=(
            P(None, "dp", "mp"),
            P(None, "dp", "mp"),
            P("mp", None),
            P(None, "mp", None),
            P(None, "mp", None),
        ),
        check_vma=False,
    )
```

```python
import jax
import jax.numpy as jnp
from jax import lax
from jax.experimental import pallas as pl
from jax.experimental.pallas import tpu as pltpu
from jax.sharding import PartitionSpec as P

HEAD_WIDTH = 64
PAIR = 2 * HEAD_WIDTH
MESH = pl.DeviceIdType.MESH
F32 = jnp.float32
BF16 = jnp.bfloat16

DP, CHIPS, CORES = 4, 4, 2


def attention_kernel(
    q_hbm, mem_in, wk_hbm, wv_hbm, g_hbm,
    att_hbm, gq_hbm, kvg_hbm, mem_hbm, gm0_hbm, gm1_hbm, gm2_hbm, gm3_hbm,
    q_v, g_v, qt_v, gt_v, att_v, gq_v, w_v, mem_ref, mg, acc, kvt, part, own, landed, kvg,
    gm_v, gm_landed,
    in_sem, w_sem, out_sem, z_send, z_recv, d_send, d_recv, s_send, s_recv,
    rs_send, rs_recv, ag_send, ag_recv, gm_sem,
):
    layers, rows, width = q_v.shape
    tokens = mem_ref.shape[0]
    quarter = mem_ref.shape[1] // DP
    mem_total = tokens * CHIPS * CORES
    i = lax.axis_index("dp")
    me = lax.axis_index("mp")
    z = me // CORES
    core = me % CORES
    sibling = z * CORES + 1 - core

    def z_peer(k):
        return {"dp": i, "mp": ((z + k) % CHIPS) * CORES + core}

    def d_peer(k):
        return {"dp": (i + k) % DP, "mp": me}

    sib = {"dp": i, "mp": sibling}

    def load_w(step):
        j = (i + DP - step) % DP
        cols = pl.ds(pl.multiple_of(j * quarter, quarter), quarter)
        return [
            pltpu.make_async_copy(
                hbm.at[:, :, cols], w_v.at[:, kv, :, cols], w_sem.at[step, kv]
            )
            for kv, hbm in enumerate((wk_hbm, wv_hbm))
        ]

    load_mem = pltpu.make_async_copy(mem_in, mem_ref, in_sem.at[2])
    load_q = pltpu.make_async_copy(q_hbm, q_v, in_sem.at[0])
    load_g = pltpu.make_async_copy(g_hbm, g_v, in_sem.at[1])
    load_mem.start()
    load_q.start()
    load_g.start()
    for step in range(DP):
        for copy in load_w(step):
            copy.start()

    barrier = pltpu.get_barrier_semaphore()
    for k in range(1, CHIPS):
        pl.semaphore_signal(barrier, inc=1, device_id=z_peer(k), device_id_type=MESH)
    for k in range(1, DP):
        pl.semaphore_signal(barrier, inc=1, device_id=d_peer(k), device_id_type=MESH)
    pl.semaphore_signal(barrier, inc=1, device_id=sib, device_id_type=MESH)
    load_mem.wait()
    pl.semaphore_wait(barrier, CHIPS + DP - 1)

    mine = pl.ds(pl.multiple_of(i * quarter, quarter), quarter)
    z_copies = []
    for k in range(1, CHIPS):
        z_copies.append(
            pltpu.make_async_remote_copy(
                src_ref=mem_ref.at[:, mine],
                dst_ref=mg.at[i, core, z],
                send_sem=z_send.at[k - 1],
                recv_sem=z_recv.at[k - 1],
                device_id=z_peer(k),
                device_id_type=MESH,
            )
        )
        z_copies[-1].start()
    mg[i, core, z] = mem_ref[:, mine]
    for copy in z_copies:
        copy.wait_recv()

    def to_sibling(step):
        j = (i + DP - step) % DP
        return pltpu.make_async_remote_copy(
            src_ref=mg.at[j, core],
            dst_ref=mg.at[j, core],
            send_sem=s_send.at[step],
            recv_sem=s_recv.at[step],
            device_id=sib,
            device_id_type=MESH,
        )

    d_copies = []
    s_copies = [to_sibling(0)]
    s_copies[0].start()
    for k in range(1, DP):
        d_copies.append(
            pltpu.make_async_remote_copy(
                src_ref=mg.at[i, core],
                dst_ref=mg.at[i, core],
                send_sem=d_send.at[k - 1],
                recv_sem=d_recv.at[k - 1],
                device_id=d_peer(k),
                device_id_type=MESH,
            )
        )
        d_copies[-1].start()

    def pair_rows(pair):
        return pl.ds(pl.multiple_of(pair * PAIR, PAIR), PAIR)

    load_q.wait()
    load_g.wait()

    @pl.loop(0, layers * DP)
    def turn(n):
        lanes = pair_rows(n % DP)
        qt_v[n // DP, lanes, :] = q_v[n // DP, :, lanes].T
        gt_v[n // DP, lanes, :] = g_v[n // DP, :, lanes].T

    acc[...] = jnp.zeros_like(acc)
    for step in range(DP):
        j = (i + DP - step) % DP
        cols = pl.ds(pl.multiple_of(j * quarter, quarter), quarter)
        if step >= 1:
            d_copies[step - 1].wait_recv()
            s_copies.append(to_sibling(step))
            s_copies[step].start()
        for copy in load_w(step):
            copy.wait()
        s_copies[step].wait_recv()

        @pl.loop(0, layers * 2)
        def project(n):
            mem_cols = mg[j].reshape(mem_total, quarter)
            acc[n // 2, n % 2] += lax.dot_general(
                w_v[n // 2, n % 2, :, cols],
                mem_cols,
                (((1,), (1,)), ((), ())),
                preferred_element_type=F32,
            )

    kvt[...] = acc[...].astype(BF16)
    for copy in z_copies + d_copies + s_copies:
        copy.wait_send()
    mem_out = pltpu.make_async_copy(mg, mem_hbm, out_sem.at[0])
    mem_out.start()

    def rs_copy(layer, t):
        return pltpu.make_async_remote_copy(
            src_ref=part.at[layer, t],
            dst_ref=landed.at[layer, t],
            send_sem=rs_send.at[layer, t],
            recv_sem=rs_recv.at[layer, t],
            device_id={"dp": (i + 1 + t) % DP, "mp": me},
            device_id_type=MESH,
        )

    def ag_copy(layer, k):
        block = kvg.at[layer, :, pair_rows(i), :]
        return pltpu.make_async_remote_copy(
            src_ref=block,
            dst_ref=block,
            send_sem=ag_send.at[layer, k - 1],
            recv_sem=ag_recv.at[layer, k - 1],
            device_id=d_peer(k),
            device_id_type=MESH,
        )

    def reduce(layer):
        total = own[layer]
        for t in range(DP - 1):
            rs_copy(layer, t).wait_recv()
            total = total + landed[layer, t].astype(F32)
        kvg[layer, :, pair_rows(i), :] = total.astype(BF16)
        for k in range(1, DP):
            ag_copy(layer, k).start()

    first_head = lax.broadcasted_iota(jnp.int32, (PAIR, mem_total), 0) < HEAD_WIDTH

    def block_diagonal(block):
        zero = jnp.zeros_like(block)
        return jnp.concatenate(
            [jnp.where(first_head, block, zero), jnp.where(first_head, zero, block)], axis=1
        )

    def own_blocks(both):
        return jnp.where(first_head, both[:, :mem_total], both[:, mem_total:])

    def attend(layer, t):
        pair = (i + 1 + t) % DP
        lanes = pair_rows(pair)
        queries = q_v[layer, :, lanes]
        grads = g_v[layer, :, lanes]
        keys = block_diagonal(kvt[layer, 0, lanes, :])
        values = block_diagonal(kvt[layer, 1, lanes, :])
        scores = jnp.dot(queries, keys, preferred_element_type=F32)
        grad_probs = jnp.dot(grads, values, preferred_element_type=F32)
        probs_b, grad_scores = [], []
        for head in range(2):
            at = slice(head * mem_total, (head + 1) * mem_total)
            s = scores[:, at]
            gp = grad_probs[:, at]
            e = jnp.exp(s - jnp.max(s, axis=-1, keepdims=True))
            probs = e * (1.0 / jnp.sum(e, axis=-1, keepdims=True))
            delta = jnp.sum(probs * gp, axis=-1, keepdims=True)
            probs_b.append(probs.astype(BF16))
            grad_scores.append((probs * (gp - delta)).astype(BF16))
        probs_b = jnp.concatenate(probs_b, axis=1)
        grad_scores = jnp.concatenate(grad_scores, axis=1)
        nt = (((1,), (1,)), ((), ()))
        att_v[layer, :, lanes] = lax.dot_general(
            probs_b, values, nt, preferred_element_type=F32
        ).astype(BF16)
        gq_v[layer, :, lanes] = lax.dot_general(
            grad_scores, keys, nt, preferred_element_type=F32
        ).astype(BF16)
        grad_keys = own_blocks(
            jnp.dot(qt_v[layer, lanes, :], grad_scores, preferred_element_type=F32)
        )
        grad_values = own_blocks(
            jnp.dot(gt_v[layer, lanes, :], probs_b, preferred_element_type=F32)
        )
        return grad_keys, grad_values

    def send_part(layer, t, grads):
        for kv in range(2):
            part[layer, t, kv] = grads[kv].astype(BF16)
        rs_copy(layer, t).start()

    @pl.loop(0, layers)
    def one_layer(layer):
        first, second = attend(layer, 0), attend(layer, 1)
        send_part(layer, 0, first)
        send_part(layer, 1, second)

        @pl.when(layer >= 1)
        def _():
            reduce(layer - 1)

        third, last = attend(layer, 2), attend(layer, 3)
        send_part(layer, 2, third)
        for kv in range(2):
            own[layer, kv] = last[kv]

    att_out = pltpu.make_async_copy(att_v, att_hbm, out_sem.at[1])
    gq_out = pltpu.make_async_copy(gq_v, gq_hbm, out_sem.at[2])
    att_out.start()
    gq_out.start()

    def add_memory_gradient(layer):
        for k in range(1, DP):
            ag_copy(layer, k).wait_recv()
        for kv in range(2):
            term = lax.dot_general(
                kvg[layer, kv],
                w_v[layer, kv, :, mine],
                (((0,), (0,)), ((), ())),
                preferred_element_type=F32,
            ).reshape(CORES, CHIPS, tokens, quarter)
            if layer == 0 and kv == 0:
                gm_v[...] = term
            else:
                gm_v[...] += term

    for layer in range(layers):
        if layer == layers - 1:
            reduce(layer)
            add_memory_gradient(layer - 1)
            add_memory_gradient(layer)
        elif layer < layers - 2:
            add_memory_gradient(layer)
    kvg_out = pltpu.make_async_copy(kvg, kvg_hbm, out_sem.at[3])
    kvg_out.start()
    gm_copy = pltpu.make_async_remote_copy(
        src_ref=gm_v.at[1 - core],
        dst_ref=gm_landed,
        send_sem=gm_sem.at[0],
        recv_sem=gm_sem.at[1],
        device_id=sib,
        device_id_type=MESH,
    )
    gm_copy.start()
    for layer in range(layers):
        for t in range(DP - 1):
            rs_copy(layer, t).wait_send()
            ag_copy(layer, t + 1).wait_send()
    gm_copy.wait()
    gm_landed[...] += gm_v[core]
    gm_outs = [
        pltpu.make_async_copy(gm_landed.at[(z + k) % CHIPS], hbm, out_sem.at[4 + k])
        for k, hbm in enumerate((gm0_hbm, gm1_hbm, gm2_hbm, gm3_hbm))
    ]
    for copy in gm_outs:
        copy.start()
    for copy in [mem_out, att_out, gq_out, kvg_out] + gm_outs:
        copy.wait()


def attention(queries, memory, w_key, w_value, grad_out):
    layers, rows, width = queries.shape
    tokens, model = memory.shape
    quarter = model // DP
    mem_total = tokens * CHIPS * CORES
    any_spec = pl.BlockSpec(memory_space=pl.ANY)
    dma = pltpu.SemaphoreType.DMA
    out_shape = (
        jax.ShapeDtypeStruct(queries.shape, BF16),
        jax.ShapeDtypeStruct(queries.shape, BF16),
        jax.ShapeDtypeStruct((layers, 2, width, mem_total), BF16),
        jax.ShapeDtypeStruct((DP, CORES, CHIPS, tokens, quarter), BF16),
    ) + (jax.ShapeDtypeStruct((tokens, quarter), F32),) * CHIPS
    return pl.pallas_call(
        attention_kernel,
        out_shape=out_shape,
        in_specs=[any_spec, pl.BlockSpec(memory_space=pltpu.HBM)] + [any_spec] * 3,
        out_specs=(any_spec,) * (4 + CHIPS),
        scratch_shapes=[
            pltpu.VMEM(queries.shape, BF16),
            pltpu.VMEM(queries.shape, BF16),
            pltpu.VMEM((layers, width, rows), BF16),
            pltpu.VMEM((layers, width, rows), BF16),
            pltpu.VMEM(queries.shape, BF16),
            pltpu.VMEM(queries.shape, BF16),
            pltpu.VMEM((layers, 2, width, model), BF16),
            pltpu.VMEM(memory.shape, BF16),
            pltpu.VMEM((DP, CORES, CHIPS, tokens, quarter), BF16),
            pltpu.VMEM((layers, 2, width, mem_total), F32),
            pltpu.VMEM((layers, 2, width, mem_total), BF16),
            pltpu.VMEM((layers, DP - 1, 2, PAIR, mem_total), BF16),
            pltpu.VMEM((layers, 2, PAIR, mem_total), F32),
            pltpu.VMEM((layers, DP - 1, 2, PAIR, mem_total), BF16),
            pltpu.VMEM((layers, 2, width, mem_total), BF16),
            pltpu.VMEM((CORES, CHIPS, tokens, quarter), F32),
            pltpu.VMEM((CHIPS, tokens, quarter), F32),
            dma((3,)),
            dma((DP, 2)),
            dma((4 + CHIPS,)),
            dma((CHIPS - 1,)),
            dma((CHIPS - 1,)),
            dma((DP - 1,)),
            dma((DP - 1,)),
            dma((DP,)),
            dma((DP,)),
            dma((layers, DP - 1)),
            dma((layers, DP - 1)),
            dma((layers, DP - 1)),
            dma((layers, DP - 1)),
            dma((2,)),
        ],
        compiler_params=pltpu.CompilerParams(
            collective_id=0, has_side_effects=True, vmem_limit_bytes=52 * 2**20
        ),
        cost_estimate=pl.CostEstimate(
            flops=8 * 10**9, bytes_accessed=35 * 10**6, transcendentals=2 * 10**6
        ),
        name="attention",
    )(queries, memory, w_key, w_value, grad_out)


def weight_kernel(kvg_ref, mem_ref, out_ref):
    quarter = mem_ref.shape[-1]
    for j in range(DP):
        out_ref[0, :, j * quarter : (j + 1) * quarter] = jnp.dot(
            kvg_ref[0, 0], mem_ref[j], preferred_element_type=F32
        )


def weight_gradient(kvg, mem, kv):
    layers, _, width, mem_total = kvg.shape
    quarter = mem.shape[-1]
    model = DP * quarter
    rows = 256
    return pl.pallas_call(
        weight_kernel,
        grid=(layers, width // rows),
        in_specs=[
            pl.BlockSpec((1, 1, rows, mem_total), lambda l, c: (l, kv, c, 0)),
            pl.BlockSpec((DP, mem_total, quarter), lambda l, c: (0, 0, 0)),
        ],
        out_specs=pl.BlockSpec((1, rows, model), lambda l, c: (l, c, 0)),
        out_shape=jax.ShapeDtypeStruct((layers, width, model), F32),
        compiler_params=pltpu.CompilerParams(vmem_limit_bytes=32 * 2**20),
        cost_estimate=pl.CostEstimate(
            flops=2 * layers * width * mem_total * model,
            bytes_accessed=4 * layers * width * model,
            transcendentals=0,
        ),
        name=("grad_w_key", "grad_w_value")[kv],
    )(kvg, mem)


def place_kernel(*refs):
    out_ref = refs[-1]
    quarter = refs[0].shape[-1]
    i = lax.axis_index("dp")
    for k, ref in enumerate(refs[:-1]):
        j = (i + DP - k) % DP
        out_ref[:, pl.ds(pl.multiple_of(j * quarter, quarter), quarter)] = ref[...]


def fused_shards(queries, memory, w_key, w_value, grad_out):
    attended, grad_queries, kvg, mem, *gm_parts = attention(
        queries, memory, w_key, w_value, grad_out
    )
    tokens, model = memory.shape
    mem = mem.reshape(DP, tokens * CHIPS * CORES, model // DP)
    gm = gm_parts[0]
    for k in range(1, CHIPS):
        ring = [
            (z * CORES + core, (z + k) % CHIPS * CORES + core)
            for z in range(CHIPS)
            for core in range(CORES)
        ]
        gm = gm + lax.ppermute(gm_parts[k], "mp", ring)
    grad_w_key = weight_gradient(kvg, mem, 0)
    grad_w_key, gm = lax.optimization_barrier((grad_w_key, gm))
    quarters = [gm] + [
        lax.ppermute(gm, "dp", [(i, (i + k) % DP) for i in range(DP)]) for k in range(1, DP)
    ]
    grad_w_value = weight_gradient(kvg, mem, 1)
    grad_memory = pl.pallas_call(
        place_kernel,
        in_specs=[pl.BlockSpec(memory_space=pltpu.VMEM)] * DP,
        out_specs=pl.BlockSpec(memory_space=pltpu.VMEM),
        out_shape=jax.ShapeDtypeStruct((tokens, model), F32),
        name="place",
    )(*quarters)
    return attended, grad_queries, grad_memory, grad_w_key, grad_w_value


def shards(queries, memory, w_key, w_value, grad_out):
    layers, rows, width = queries.shape
    heads_dev = width // HEAD_WIDTH
    mem_all = lax.all_gather(memory, "mp", axis=0, tiled=True)
    mem_total = mem_all.shape[0]
    keys = jnp.einsum("md,lcd->lmc", mem_all, w_key, preferred_element_type=jnp.float32).astype(
        jnp.bfloat16
    )
    values = jnp.einsum("md,lcd->lmc", mem_all, w_value, preferred_element_type=jnp.float32).astype(
        jnp.bfloat16
    )
    per_head_queries = queries.reshape(layers, rows, heads_dev, HEAD_WIDTH)
    per_head_keys = keys.reshape(layers, mem_total, heads_dev, HEAD_WIDTH)
    per_head_values = values.reshape(layers, mem_total, heads_dev, HEAD_WIDTH)
    head_output_gradient = grad_out.reshape(layers, rows, heads_dev, HEAD_WIDTH)
    attention_logits = jnp.einsum(
        "lrhd,lmhd->lhrm", per_head_queries, per_head_keys, preferred_element_type=jnp.float32
    )
    row_max = jnp.max(attention_logits, axis=-1, keepdims=True)
    exp_scores = jnp.exp(attention_logits - row_max)
    attn_probs = exp_scores / jnp.sum(exp_scores, axis=-1, keepdims=True)
    batch_probabilities = attn_probs.astype(jnp.bfloat16)
    attended = (
        jnp.einsum(
            "lhrm,lmhd->lrhd",
            batch_probabilities,
            per_head_values,
            preferred_element_type=jnp.float32,
        )
        .reshape(layers, rows, width)
        .astype(jnp.bfloat16)
    )
    probability_gradient = jnp.einsum(
        "lrhd,lmhd->lhrm", head_output_gradient, per_head_values, preferred_element_type=jnp.float32
    )
    row_delta = jnp.sum(attn_probs * probability_gradient, axis=-1, keepdims=True)
    logit_gradient = (attn_probs * (probability_gradient - row_delta)).astype(jnp.bfloat16)
    grad_queries = (
        jnp.einsum(
            "lhrm,lmhd->lrhd", logit_gradient, per_head_keys, preferred_element_type=jnp.float32
        )
        .reshape(layers, rows, width)
        .astype(jnp.bfloat16)
    )
    key_part = jnp.einsum(
        "lhrm,lrhd->lmhd", logit_gradient, per_head_queries, preferred_element_type=jnp.float32
    ).reshape(layers, mem_total, width)
    value_part = jnp.einsum(
        "lhrm,lrhd->lmhd",
        batch_probabilities,
        head_output_gradient,
        preferred_element_type=jnp.float32,
    ).reshape(layers, mem_total, width)
    key_sum, value_sum = lax.psum((key_part, value_part), "dp")
    key_gradient = key_sum.astype(jnp.bfloat16)
    value_gradient = value_sum.astype(jnp.bfloat16)
    grad_w_key = jnp.einsum(
        "lmc,md->lcd", key_gradient, mem_all, preferred_element_type=jnp.float32
    )
    grad_w_value = jnp.einsum(
        "lmc,md->lcd", value_gradient, mem_all, preferred_element_type=jnp.float32
    )
    grad_memory = lax.psum_scatter(
        jnp.einsum("lmc,lcd->md", key_gradient, w_key, preferred_element_type=jnp.float32)
        + jnp.einsum("lmc,lcd->md", value_gradient, w_value, preferred_element_type=jnp.float32),
        "mp",
        scatter_dimension=0,
        tiled=True,
    )
    return (attended, grad_queries, grad_memory, grad_w_key, grad_w_value)


def solution(mesh):
    def choose(queries, memory, w_key, w_value, grad_out):
        fits = (
            mesh.shape["dp"] == DP
            and mesh.shape["mp"] == CHIPS * CORES
            and queries.shape[2] == DP * PAIR
            and memory.shape[0] == 16
            and memory.shape[1] % (DP * 128) == 0
        )
        run = fused_shards if fits else shards
        return run(queries, memory, w_key, w_value, grad_out)

    return jax.shard_map(
        choose,
        mesh=mesh,
        in_specs=(
            P(None, "dp", "mp"),
            P("mp", None),
            P(None, "mp", None),
            P(None, "mp", None),
            P(None, "dp", "mp"),
        ),
        out_specs=(
            P(None, "dp", "mp"),
            P(None, "dp", "mp"),
            P("mp", None),
            P(None, "mp", None),
            P(None, "mp", None),
        ),
        check_vma=False,
    )
```

```python
import jax
import jax.numpy as jnp
from jax import lax
from jax.experimental import pallas as pl
from jax.experimental.pallas import tpu as pltpu
from jax.sharding import PartitionSpec as P

HEAD_WIDTH = 64
PAIR = 2 * HEAD_WIDTH
MESH = pl.DeviceIdType.MESH
F32 = jnp.float32
BF16 = jnp.bfloat16

DP, CHIPS, CORES = 4, 4, 2


def attention_kernel(
    q_hbm, mem_in, wk_hbm, wv_hbm, g_hbm,
    att_hbm, gq_hbm, kvg_hbm, mem_hbm, gm0_hbm, gm1_hbm, gm2_hbm, gm3_hbm,
    q_v, g_v, qt_v, gt_v, att_t, gq_t, w_v, mem_ref, mg, acc, kvt, part, own, landed, kvg,
    gm_v, gm_landed,
    in_sem, w_sem, out_sem, z_send, z_recv, d_send, d_recv, s_send, s_recv,
    rs_send, rs_recv, ag_send, ag_recv, gm_sem,
):
    layers, rows, width = q_v.shape
    tokens = mem_ref.shape[0]
    quarter = mem_ref.shape[1] // DP
    mem_total = tokens * CHIPS * CORES
    i = lax.axis_index("dp")
    me = lax.axis_index("mp")
    z = me // CORES
    core = me % CORES
    sibling = z * CORES + 1 - core

    def z_peer(k):
        return {"dp": i, "mp": ((z + k) % CHIPS) * CORES + core}

    def d_peer(k):
        return {"dp": (i + k) % DP, "mp": me}

    sib = {"dp": i, "mp": sibling}

    def load_w(step):
        j = (i + DP - step) % DP
        cols = pl.ds(pl.multiple_of(j * quarter, quarter), quarter)
        return [
            pltpu.make_async_copy(
                hbm.at[:, :, cols], w_v.at[:, kv, :, cols], w_sem.at[step, kv]
            )
            for kv, hbm in enumerate((wk_hbm, wv_hbm))
        ]

    load_mem = pltpu.make_async_copy(mem_in, mem_ref, in_sem.at[2])
    load_q = pltpu.make_async_copy(q_hbm, q_v, in_sem.at[0])
    load_g = pltpu.make_async_copy(g_hbm, g_v, in_sem.at[1])
    load_mem.start()
    load_q.start()
    load_g.start()
    for step in range(DP):
        for copy in load_w(step):
            copy.start()

    barrier = pltpu.get_barrier_semaphore()
    for k in range(1, CHIPS):
        pl.semaphore_signal(barrier, inc=1, device_id=z_peer(k), device_id_type=MESH)
    for k in range(1, DP):
        pl.semaphore_signal(barrier, inc=1, device_id=d_peer(k), device_id_type=MESH)
    pl.semaphore_signal(barrier, inc=1, device_id=sib, device_id_type=MESH)
    load_mem.wait()
    pl.semaphore_wait(barrier, CHIPS + DP - 1)

    mine = pl.ds(pl.multiple_of(i * quarter, quarter), quarter)
    z_copies = []
    for k in range(1, CHIPS):
        z_copies.append(
            pltpu.make_async_remote_copy(
                src_ref=mem_ref.at[:, mine],
                dst_ref=mg.at[i, core, z],
                send_sem=z_send.at[k - 1],
                recv_sem=z_recv.at[k - 1],
                device_id=z_peer(k),
                device_id_type=MESH,
            )
        )
        z_copies[-1].start()
    mg[i, core, z] = mem_ref[:, mine]
    for copy in z_copies:
        copy.wait_recv()

    def to_sibling(step):
        j = (i + DP - step) % DP
        return pltpu.make_async_remote_copy(
            src_ref=mg.at[j, core],
            dst_ref=mg.at[j, core],
            send_sem=s_send.at[step],
            recv_sem=s_recv.at[step],
            device_id=sib,
            device_id_type=MESH,
        )

    d_copies = []
    s_copies = [to_sibling(0)]
    s_copies[0].start()
    for k in range(1, DP):
        d_copies.append(
            pltpu.make_async_remote_copy(
                src_ref=mg.at[i, core],
                dst_ref=mg.at[i, core],
                send_sem=d_send.at[k - 1],
                recv_sem=d_recv.at[k - 1],
                device_id=d_peer(k),
                device_id_type=MESH,
            )
        )
        d_copies[-1].start()

    def pair_rows(pair):
        return pl.ds(pl.multiple_of(pair * PAIR, PAIR), PAIR)

    load_q.wait()
    load_g.wait()

    @pl.loop(0, layers * DP)
    def turn(n):
        lanes = pair_rows(n % DP)
        qt_v[n // DP, lanes, :] = q_v[n // DP, :, lanes].T
        gt_v[n // DP, lanes, :] = g_v[n // DP, :, lanes].T

    acc[...] = jnp.zeros_like(acc)
    for step in range(DP):
        j = (i + DP - step) % DP
        cols = pl.ds(pl.multiple_of(j * quarter, quarter), quarter)
        if step >= 1:
            d_copies[step - 1].wait_recv()
            s_copies.append(to_sibling(step))
            s_copies[step].start()
        for copy in load_w(step):
            copy.wait()
        s_copies[step].wait_recv()

        @pl.loop(0, layers * 2)
        def project(n):
            mem_cols = mg[j].reshape(mem_total, quarter)
            acc[n // 2, n % 2] += lax.dot_general(
                w_v[n // 2, n % 2, :, cols],
                mem_cols,
                (((1,), (1,)), ((), ())),
                preferred_element_type=F32,
            )

    kvt[...] = acc[...].astype(BF16)
    for copy in z_copies + d_copies + s_copies:
        copy.wait_send()
    mem_out = pltpu.make_async_copy(mg, mem_hbm, out_sem.at[0])
    mem_out.start()

    def rs_copy(layer, t):
        return pltpu.make_async_remote_copy(
            src_ref=part.at[layer, t],
            dst_ref=landed.at[layer, t],
            send_sem=rs_send.at[layer, t],
            recv_sem=rs_recv.at[layer, t],
            device_id={"dp": (i + 1 + t) % DP, "mp": me},
            device_id_type=MESH,
        )

    def ag_copy(layer, k):
        block = kvg.at[layer, :, pair_rows(i), :]
        return pltpu.make_async_remote_copy(
            src_ref=block,
            dst_ref=block,
            send_sem=ag_send.at[layer, k - 1],
            recv_sem=ag_recv.at[layer, k - 1],
            device_id=d_peer(k),
            device_id_type=MESH,
        )

    def reduce(layer):
        total = own[layer]
        for t in range(DP - 1):
            rs_copy(layer, t).wait_recv()
            total = total + landed[layer, t].astype(F32)
        kvg[layer, :, pair_rows(i), :] = total.astype(BF16)
        for k in range(1, DP):
            ag_copy(layer, k).start()

    def head_masks(axis):
        return lax.broadcasted_iota(jnp.int32, (PAIR, PAIR), axis) < HEAD_WIDTH

    first_row, first_lane = head_masks(0), head_masks(1)

    def split_heads(block, mask, axis):
        zero = jnp.zeros_like(block)
        return jnp.concatenate(
            [jnp.where(mask, block, zero), jnp.where(mask, zero, block)], axis=axis
        )

    def own_blocks(both):
        return jnp.where(first_row, both[:, :mem_total], both[:, mem_total:])

    def dot_nt(lhs, rhs):
        return lax.dot_general(lhs, rhs, (((1,), (1,)), ((), ())), preferred_element_type=F32)

    def attend(layer, t):
        lanes = pair_rows((i + 1 + t) % DP)
        queries, grads = qt_v[layer, lanes, :], gt_v[layer, lanes, :]
        keys, values = kvt[layer, 0, lanes, :], kvt[layer, 1, lanes, :]
        scores = jnp.dot(
            split_heads(keys.T, first_lane, 0), queries, preferred_element_type=F32
        )
        grad_probs = jnp.dot(
            split_heads(values.T, first_lane, 0), grads, preferred_element_type=F32
        )
        probs_b, grad_scores = [], []
        for head in range(2):
            probs_row, grads_row = [], []
            for chunk in range(rows // 128):
                at = (
                    slice(head * mem_total, (head + 1) * mem_total),
                    slice(chunk * 128, (chunk + 1) * 128),
                )
                s, gp = scores[at], grad_probs[at]
                e = jnp.exp(s - jnp.max(s, axis=0, keepdims=True))
                scale = 1.0 / jnp.sum(e, axis=0, keepdims=True)
                delta = jnp.sum(e * gp, axis=0, keepdims=True) * scale
                probs = e * scale
                probs_row.append(probs.astype(BF16))
                grads_row.append((probs * (gp - delta)).astype(BF16))
            probs_b.append(jnp.concatenate(probs_row, axis=1))
            grad_scores.append(jnp.concatenate(grads_row, axis=1))
        probs_b = jnp.concatenate(probs_b, axis=0)
        grad_scores = jnp.concatenate(grad_scores, axis=0)
        att_t[layer, lanes, :] = jnp.dot(
            split_heads(values, first_row, 1), probs_b, preferred_element_type=F32
        ).astype(BF16)
        gq_t[layer, lanes, :] = jnp.dot(
            split_heads(keys, first_row, 1), grad_scores, preferred_element_type=F32
        ).astype(BF16)
        return own_blocks(dot_nt(queries, grad_scores)), own_blocks(dot_nt(grads, probs_b))

    def send_part(layer, t, grads):
        for kv in range(2):
            part[layer, t, kv] = grads[kv].astype(BF16)
        rs_copy(layer, t).start()

    @pl.loop(0, layers)
    def one_layer(layer):
        first, second = attend(layer, 0), attend(layer, 1)
        send_part(layer, 0, first)
        send_part(layer, 1, second)

        @pl.when(layer >= 1)
        def _():
            reduce(layer - 1)

        third, last = attend(layer, 2), attend(layer, 3)
        send_part(layer, 2, third)
        for kv in range(2):
            own[layer, kv] = last[kv]

    def add_memory_gradient(layer):
        for k in range(1, DP):
            ag_copy(layer, k).wait_recv()
        for kv in range(2):
            term = lax.dot_general(
                kvg[layer, kv],
                w_v[layer, kv, :, mine],
                (((0,), (0,)), ((), ())),
                preferred_element_type=F32,
            ).reshape(CORES, CHIPS, tokens, quarter)
            if layer == 0 and kv == 0:
                gm_v[...] = term
            else:
                gm_v[...] += term

    for layer in range(layers - 2):
        add_memory_gradient(layer)
    reduce(layers - 1)

    @pl.loop(0, layers * DP)
    def turn_back(n):
        lanes = pair_rows(n % DP)
        q_v[n // DP, :, lanes] = att_t[n // DP, lanes, :].T
        g_v[n // DP, :, lanes] = gq_t[n // DP, lanes, :].T

    att_out = pltpu.make_async_copy(q_v, att_hbm, out_sem.at[1])
    gq_out = pltpu.make_async_copy(g_v, gq_hbm, out_sem.at[2])
    att_out.start()
    gq_out.start()
    for layer in range(max(layers - 2, 0), layers):
        add_memory_gradient(layer)
    kvg_out = pltpu.make_async_copy(kvg, kvg_hbm, out_sem.at[3])
    kvg_out.start()
    gm_copy = pltpu.make_async_remote_copy(
        src_ref=gm_v.at[1 - core],
        dst_ref=gm_landed,
        send_sem=gm_sem.at[0],
        recv_sem=gm_sem.at[1],
        device_id=sib,
        device_id_type=MESH,
    )
    gm_copy.start()
    for layer in range(layers):
        for t in range(DP - 1):
            rs_copy(layer, t).wait_send()
            ag_copy(layer, t + 1).wait_send()
    gm_copy.wait()
    gm_landed[...] += gm_v[core]
    gm_outs = [
        pltpu.make_async_copy(gm_landed.at[(z + k) % CHIPS], hbm, out_sem.at[4 + k])
        for k, hbm in enumerate((gm0_hbm, gm1_hbm, gm2_hbm, gm3_hbm))
    ]
    for copy in gm_outs:
        copy.start()
    for copy in [mem_out, att_out, gq_out, kvg_out] + gm_outs:
        copy.wait()


def attention(queries, memory, w_key, w_value, grad_out):
    layers, rows, width = queries.shape
    tokens, model = memory.shape
    quarter = model // DP
    mem_total = tokens * CHIPS * CORES
    any_spec = pl.BlockSpec(memory_space=pl.ANY)
    dma = pltpu.SemaphoreType.DMA
    out_shape = (
        jax.ShapeDtypeStruct(queries.shape, BF16),
        jax.ShapeDtypeStruct(queries.shape, BF16),
        jax.ShapeDtypeStruct((layers, 2, width, mem_total), BF16),
        jax.ShapeDtypeStruct((DP, CORES, CHIPS, tokens, quarter), BF16),
    ) + (jax.ShapeDtypeStruct((tokens, quarter), F32),) * CHIPS
    return pl.pallas_call(
        attention_kernel,
        out_shape=out_shape,
        in_specs=[any_spec, pl.BlockSpec(memory_space=pltpu.HBM)] + [any_spec] * 3,
        out_specs=(any_spec,) * (4 + CHIPS),
        scratch_shapes=[
            pltpu.VMEM(queries.shape, BF16),
            pltpu.VMEM(queries.shape, BF16),
            pltpu.VMEM((layers, width, rows), BF16),
            pltpu.VMEM((layers, width, rows), BF16),
            pltpu.VMEM((layers, width, rows), BF16),
            pltpu.VMEM((layers, width, rows), BF16),
            pltpu.VMEM((layers, 2, width, model), BF16),
            pltpu.VMEM(memory.shape, BF16),
            pltpu.VMEM((DP, CORES, CHIPS, tokens, quarter), BF16),
            pltpu.VMEM((layers, 2, width, mem_total), F32),
            pltpu.VMEM((layers, 2, width, mem_total), BF16),
            pltpu.VMEM((layers, DP - 1, 2, PAIR, mem_total), BF16),
            pltpu.VMEM((layers, 2, PAIR, mem_total), F32),
            pltpu.VMEM((layers, DP - 1, 2, PAIR, mem_total), BF16),
            pltpu.VMEM((layers, 2, width, mem_total), BF16),
            pltpu.VMEM((CORES, CHIPS, tokens, quarter), F32),
            pltpu.VMEM((CHIPS, tokens, quarter), F32),
            dma((3,)),
            dma((DP, 2)),
            dma((4 + CHIPS,)),
            dma((CHIPS - 1,)),
            dma((CHIPS - 1,)),
            dma((DP - 1,)),
            dma((DP - 1,)),
            dma((DP,)),
            dma((DP,)),
            dma((layers, DP - 1)),
            dma((layers, DP - 1)),
            dma((layers, DP - 1)),
            dma((layers, DP - 1)),
            dma((2,)),
        ],
        compiler_params=pltpu.CompilerParams(
            collective_id=0, has_side_effects=True, vmem_limit_bytes=52 * 2**20
        ),
        cost_estimate=pl.CostEstimate(
            flops=8 * 10**9, bytes_accessed=35 * 10**6, transcendentals=2 * 10**6
        ),
        name="attention",
    )(queries, memory, w_key, w_value, grad_out)


def weight_kernel(kvg_ref, mem_ref, out_ref):
    quarter = mem_ref.shape[-1]
    for j in range(DP):
        out_ref[0, :, j * quarter : (j + 1) * quarter] = jnp.dot(
            kvg_ref[0, 0], mem_ref[j], preferred_element_type=F32
        )


def weight_gradient(kvg, mem, kv):
    layers, _, width, mem_total = kvg.shape
    quarter = mem.shape[-1]
    model = DP * quarter
    rows = 128
    return pl.pallas_call(
        weight_kernel,
        grid=(layers, width // rows),
        in_specs=[
            pl.BlockSpec((1, 1, rows, mem_total), lambda l, c: (l, kv, c, 0)),
            pl.BlockSpec((DP, mem_total, quarter), lambda l, c: (0, 0, 0)),
        ],
        out_specs=pl.BlockSpec((1, rows, model), lambda l, c: (l, c, 0)),
        out_shape=jax.ShapeDtypeStruct((layers, width, model), F32),
        compiler_params=pltpu.CompilerParams(vmem_limit_bytes=32 * 2**20),
        cost_estimate=pl.CostEstimate(
            flops=2 * layers * width * mem_total * model,
            bytes_accessed=4 * layers * width * model,
            transcendentals=0,
        ),
        name=("grad_w_key", "grad_w_value")[kv],
    )(kvg, mem)


def place_kernel(*refs):
    out_ref = refs[-1]
    quarter = refs[0].shape[-1]
    i = lax.axis_index("dp")
    for k, ref in enumerate(refs[:-1]):
        j = (i + DP - k) % DP
        out_ref[:, pl.ds(pl.multiple_of(j * quarter, quarter), quarter)] = ref[...]


def fused_shards(queries, memory, w_key, w_value, grad_out):
    attended, grad_queries, kvg, mem, *gm_parts = attention(
        queries, memory, w_key, w_value, grad_out
    )
    tokens, model = memory.shape
    mem = mem.reshape(DP, tokens * CHIPS * CORES, model // DP)
    gm = gm_parts[0]
    for k in range(1, CHIPS):
        ring = [
            (z * CORES + core, (z + k) % CHIPS * CORES + core)
            for z in range(CHIPS)
            for core in range(CORES)
        ]
        gm = gm + lax.ppermute(gm_parts[k], "mp", ring)
    grad_w_key = weight_gradient(kvg, mem, 0)
    grad_w_key, gm = lax.optimization_barrier((grad_w_key, gm))
    quarters = [gm] + [
        lax.ppermute(gm, "dp", [(i, (i + k) % DP) for i in range(DP)]) for k in range(1, DP)
    ]
    grad_w_value = weight_gradient(kvg, mem, 1)
    grad_memory = pl.pallas_call(
        place_kernel,
        in_specs=[pl.BlockSpec(memory_space=pltpu.VMEM)] * DP,
        out_specs=pl.BlockSpec(memory_space=pltpu.VMEM),
        out_shape=jax.ShapeDtypeStruct((tokens, model), F32),
        name="place",
    )(*quarters)
    return attended, grad_queries, grad_memory, grad_w_key, grad_w_value


def shards(queries, memory, w_key, w_value, grad_out):
    layers, rows, width = queries.shape
    heads_dev = width // HEAD_WIDTH
    mem_all = lax.all_gather(memory, "mp", axis=0, tiled=True)
    mem_total = mem_all.shape[0]
    keys = jnp.einsum("md,lcd->lmc", mem_all, w_key, preferred_element_type=jnp.float32).astype(
        jnp.bfloat16
    )
    values = jnp.einsum("md,lcd->lmc", mem_all, w_value, preferred_element_type=jnp.float32).astype(
        jnp.bfloat16
    )
    per_head_queries = queries.reshape(layers, rows, heads_dev, HEAD_WIDTH)
    per_head_keys = keys.reshape(layers, mem_total, heads_dev, HEAD_WIDTH)
    per_head_values = values.reshape(layers, mem_total, heads_dev, HEAD_WIDTH)
    head_output_gradient = grad_out.reshape(layers, rows, heads_dev, HEAD_WIDTH)
    attention_logits = jnp.einsum(
        "lrhd,lmhd->lhrm", per_head_queries, per_head_keys, preferred_element_type=jnp.float32
    )
    row_max = jnp.max(attention_logits, axis=-1, keepdims=True)
    exp_scores = jnp.exp(attention_logits - row_max)
    attn_probs = exp_scores / jnp.sum(exp_scores, axis=-1, keepdims=True)
    batch_probabilities = attn_probs.astype(jnp.bfloat16)
    attended = (
        jnp.einsum(
            "lhrm,lmhd->lrhd",
            batch_probabilities,
            per_head_values,
            preferred_element_type=jnp.float32,
        )
        .reshape(layers, rows, width)
        .astype(jnp.bfloat16)
    )
    probability_gradient = jnp.einsum(
        "lrhd,lmhd->lhrm", head_output_gradient, per_head_values, preferred_element_type=jnp.float32
    )
    row_delta = jnp.sum(attn_probs * probability_gradient, axis=-1, keepdims=True)
    logit_gradient = (attn_probs * (probability_gradient - row_delta)).astype(jnp.bfloat16)
    grad_queries = (
        jnp.einsum(
            "lhrm,lmhd->lrhd", logit_gradient, per_head_keys, preferred_element_type=jnp.float32
        )
        .reshape(layers, rows, width)
        .astype(jnp.bfloat16)
    )
    key_part = jnp.einsum(
        "lhrm,lrhd->lmhd", logit_gradient, per_head_queries, preferred_element_type=jnp.float32
    ).reshape(layers, mem_total, width)
    value_part = jnp.einsum(
        "lhrm,lrhd->lmhd",
        batch_probabilities,
        head_output_gradient,
        preferred_element_type=jnp.float32,
    ).reshape(layers, mem_total, width)
    key_sum, value_sum = lax.psum((key_part, value_part), "dp")
    key_gradient = key_sum.astype(jnp.bfloat16)
    value_gradient = value_sum.astype(jnp.bfloat16)
    grad_w_key = jnp.einsum(
        "lmc,md->lcd", key_gradient, mem_all, preferred_element_type=jnp.float32
    )
    grad_w_value = jnp.einsum(
        "lmc,md->lcd", value_gradient, mem_all, preferred_element_type=jnp.float32
    )
    grad_memory = lax.psum_scatter(
        jnp.einsum("lmc,lcd->md", key_gradient, w_key, preferred_element_type=jnp.float32)
        + jnp.einsum("lmc,lcd->md", value_gradient, w_value, preferred_element_type=jnp.float32),
        "mp",
        scatter_dimension=0,
        tiled=True,
    )
    return (attended, grad_queries, grad_memory, grad_w_key, grad_w_value)


def solution(mesh):
    def choose(queries, memory, w_key, w_value, grad_out):
        fits = (
            mesh.shape["dp"] == DP
            and mesh.shape["mp"] == CHIPS * CORES
            and queries.shape[2] == DP * PAIR
            and queries.shape[1] % (128 * DP) == 0
            and memory.shape[0] == PAIR // (CHIPS * CORES)
            and memory.shape[1] % (DP * 128) == 0
        )
        run = fused_shards if fits else shards
        return run(queries, memory, w_key, w_value, grad_out)

    return jax.shard_map(
        choose,
        mesh=mesh,
        in_specs=(
            P(None, "dp", "mp"),
            P("mp", None),
            P(None, "mp", None),
            P(None, "mp", None),
            P(None, "dp", "mp"),
        ),
        out_specs=(
            P(None, "dp", "mp"),
            P(None, "dp", "mp"),
            P("mp", None),
            P(None, "mp", None),
            P(None, "mp", None),
        ),
        check_vma=False,
    )
```

```python
import jax
import jax.numpy as jnp
from jax import lax
from jax.experimental import pallas as pl
from jax.experimental.pallas import tpu as pltpu
from jax.sharding import PartitionSpec as P

HEAD_WIDTH = 64
PAIR = 2 * HEAD_WIDTH
MESH = pl.DeviceIdType.MESH
F32 = jnp.float32
BF16 = jnp.bfloat16

DP, CHIPS, CORES = 4, 4, 2


def attention_kernel(
    q_hbm, mem_in, wk_hbm, wv_hbm, g_hbm,
    att_hbm, gq_hbm, kvg_hbm, mem_hbm, gm0_hbm, gm1_hbm, gm2_hbm, gm3_hbm,
    q_v, g_v, qt_v, gt_v, att_t, gq_t, w_v, mem_ref, mg, mt, acc, kvt, part, own, landed, kvg,
    gm_v, gm_landed,
    in_sem, w_sem, out_sem, z_send, z_recv, d_send, d_recv, s_send, s_recv,
    rs_send, rs_recv, ag_send, ag_recv, gm_sem,
):
    layers, rows, width = q_v.shape
    tokens = mem_ref.shape[0]
    quarter = mem_ref.shape[1] // DP
    mem_total = tokens * CHIPS * CORES
    i = lax.axis_index("dp")
    me = lax.axis_index("mp")
    z = me // CORES
    core = me % CORES
    sibling = z * CORES + 1 - core

    def z_peer(k):
        return {"dp": i, "mp": ((z + k) % CHIPS) * CORES + core}

    def d_peer(k):
        return {"dp": (i + k) % DP, "mp": me}

    sib = {"dp": i, "mp": sibling}

    def load_w(step):
        j = (i + DP - step) % DP
        cols = pl.ds(pl.multiple_of(j * quarter, quarter), quarter)
        return [
            pltpu.make_async_copy(
                hbm.at[:, :, cols], w_v.at[:, kv, :, cols], w_sem.at[step, kv]
            )
            for kv, hbm in enumerate((wk_hbm, wv_hbm))
        ]

    load_mem = pltpu.make_async_copy(mem_in, mem_ref, in_sem.at[2])
    load_q = pltpu.make_async_copy(q_hbm, q_v, in_sem.at[0])
    load_g = pltpu.make_async_copy(g_hbm, g_v, in_sem.at[1])
    load_mem.start()
    load_q.start()
    load_g.start()
    for step in range(DP):
        for copy in load_w(step):
            copy.start()

    barrier = pltpu.get_barrier_semaphore()
    for k in range(1, CHIPS):
        pl.semaphore_signal(barrier, inc=1, device_id=z_peer(k), device_id_type=MESH)
    for k in range(1, DP):
        pl.semaphore_signal(barrier, inc=1, device_id=d_peer(k), device_id_type=MESH)
    pl.semaphore_signal(barrier, inc=1, device_id=sib, device_id_type=MESH)
    load_mem.wait()
    pl.semaphore_wait(barrier, CHIPS + DP - 1)

    mine = pl.ds(pl.multiple_of(i * quarter, quarter), quarter)
    z_copies = []
    for k in range(1, CHIPS):
        z_copies.append(
            pltpu.make_async_remote_copy(
                src_ref=mem_ref.at[:, mine],
                dst_ref=mg.at[i, core, z],
                send_sem=z_send.at[k - 1],
                recv_sem=z_recv.at[k - 1],
                device_id=z_peer(k),
                device_id_type=MESH,
            )
        )
        z_copies[-1].start()
    mg[i, core, z] = mem_ref[:, mine]
    for copy in z_copies:
        copy.wait_recv()

    def to_sibling(step):
        j = (i + DP - step) % DP
        return pltpu.make_async_remote_copy(
            src_ref=mg.at[j, core],
            dst_ref=mg.at[j, core],
            send_sem=s_send.at[step],
            recv_sem=s_recv.at[step],
            device_id=sib,
            device_id_type=MESH,
        )

    d_copies = []
    s_copies = [to_sibling(0)]
    s_copies[0].start()
    for k in range(1, DP):
        d_copies.append(
            pltpu.make_async_remote_copy(
                src_ref=mg.at[i, core],
                dst_ref=mg.at[i, core],
                send_sem=d_send.at[k - 1],
                recv_sem=d_recv.at[k - 1],
                device_id=d_peer(k),
                device_id_type=MESH,
            )
        )
        d_copies[-1].start()

    def pair_rows(pair):
        return pl.ds(pl.multiple_of(pair * PAIR, PAIR), PAIR)

    load_q.wait()
    load_g.wait()

    @pl.loop(0, layers * DP)
    def turn(n):
        lanes = pair_rows(n % DP)
        qt_v[n // DP, lanes, :] = q_v[n // DP, :, lanes].T
        gt_v[n // DP, lanes, :] = g_v[n // DP, :, lanes].T

    def columns(step):
        return pl.ds(pl.multiple_of((i + DP - step) % DP * quarter, quarter), quarter)

    def project(layer, kv, step):
        return jnp.dot(w_v[layer, kv, :, columns(step)], mt[step], preferred_element_type=F32)

    for step in range(DP):
        if step >= 1:
            d_copies[step - 1].wait_recv()
            s_copies.append(to_sibling(step))
            s_copies[step].start()
        for copy in load_w(step):
            copy.wait()
        s_copies[step].wait_recv()
        mt[step] = mg[(i + DP - step) % DP].reshape(mem_total, quarter).T
        if step == 0:

            @pl.loop(0, layers * 2)
            def first_quarter(n):
                acc[n // 2, n % 2] = project(n // 2, n % 2, 0)

        elif step < DP - 1:

            @pl.loop(0, 2)
            def layer_0(kv):
                acc[0, kv] += project(0, kv, step)

        else:

            @pl.loop(0, 2)
            def layer_0_last(kv):
                kvt[0, kv] = (acc[0, kv] + project(0, kv, step)).astype(BF16)

    def finish_projection(layer):
        @pl.loop(0, 2)
        def one(kv):
            total = acc[layer, kv]
            for step in range(1, DP):
                total = total + project(layer, kv, step)
            kvt[layer, kv] = total.astype(BF16)

    mem_out = pltpu.make_async_copy(mg, mem_hbm, out_sem.at[0])
    mem_out.start()

    def rs_copy(layer, t):
        return pltpu.make_async_remote_copy(
            src_ref=part.at[layer, t],
            dst_ref=landed.at[layer, t],
            send_sem=rs_send.at[layer, t],
            recv_sem=rs_recv.at[layer, t],
            device_id={"dp": (i + 1 + t) % DP, "mp": me},
            device_id_type=MESH,
        )

    def ag_copy(layer, k):
        block = kvg.at[layer, :, pair_rows(i), :]
        return pltpu.make_async_remote_copy(
            src_ref=block,
            dst_ref=block,
            send_sem=ag_send.at[layer, k - 1],
            recv_sem=ag_recv.at[layer, k - 1],
            device_id=d_peer(k),
            device_id_type=MESH,
        )

    def reduce(layer):
        total = own[layer]
        for t in range(DP - 1):
            rs_copy(layer, t).wait_recv()
            total = total + landed[layer, t].astype(F32)
        kvg[layer, :, pair_rows(i), :] = total.astype(BF16)
        for k in range(1, DP):
            ag_copy(layer, k).start()

    def head_masks(axis):
        return lax.broadcasted_iota(jnp.int32, (PAIR, PAIR), axis) < HEAD_WIDTH

    first_row, first_lane = head_masks(0), head_masks(1)

    def split_heads(block, mask, axis):
        zero = jnp.zeros_like(block)
        return jnp.concatenate(
            [jnp.where(mask, block, zero), jnp.where(mask, zero, block)], axis=axis
        )

    def own_blocks(both):
        return jnp.where(first_row, both[:, :mem_total], both[:, mem_total:])

    def dot_nt(lhs, rhs):
        return lax.dot_general(lhs, rhs, (((1,), (1,)), ((), ())), preferred_element_type=F32)

    def attend(layer, t):
        lanes = pair_rows((i + 1 + t) % DP)
        queries, grads = qt_v[layer, lanes, :], gt_v[layer, lanes, :]
        keys, values = kvt[layer, 0, lanes, :], kvt[layer, 1, lanes, :]
        scores = jnp.dot(
            split_heads(keys.T, first_lane, 0), queries, preferred_element_type=F32
        )
        grad_probs = jnp.dot(
            split_heads(values.T, first_lane, 0), grads, preferred_element_type=F32
        )
        probs_b, grad_scores = [], []
        for head in range(2):
            probs_row, grads_row = [], []
            for chunk in range(rows // 128):
                at = (
                    slice(head * mem_total, (head + 1) * mem_total),
                    slice(chunk * 128, (chunk + 1) * 128),
                )
                s, gp = scores[at], grad_probs[at]
                e = jnp.exp(s - jnp.max(s, axis=0, keepdims=True))
                scale = 1.0 / jnp.sum(e, axis=0, keepdims=True)
                delta = jnp.sum(e * gp, axis=0, keepdims=True) * scale
                probs = e * scale
                probs_row.append(probs.astype(BF16))
                grads_row.append((probs * (gp - delta)).astype(BF16))
            probs_b.append(jnp.concatenate(probs_row, axis=1))
            grad_scores.append(jnp.concatenate(grads_row, axis=1))
        probs_b = jnp.concatenate(probs_b, axis=0)
        grad_scores = jnp.concatenate(grad_scores, axis=0)
        att_t[layer, lanes, :] = jnp.dot(
            split_heads(values, first_row, 1), probs_b, preferred_element_type=F32
        ).astype(BF16)
        gq_t[layer, lanes, :] = jnp.dot(
            split_heads(keys, first_row, 1), grad_scores, preferred_element_type=F32
        ).astype(BF16)
        return own_blocks(dot_nt(queries, grad_scores)), own_blocks(dot_nt(grads, probs_b))

    def send_part(layer, t, grads):
        for kv in range(2):
            part[layer, t, kv] = grads[kv].astype(BF16)
        rs_copy(layer, t).start()

    @pl.loop(0, layers)
    def one_layer(layer):
        @pl.when(layer >= 1)
        def _():
            finish_projection(layer)
            reduce(layer - 1)

        first, second = attend(layer, 0), attend(layer, 1)
        send_part(layer, 0, first)
        send_part(layer, 1, second)
        third, last = attend(layer, 2), attend(layer, 3)
        send_part(layer, 2, third)
        for kv in range(2):
            own[layer, kv] = last[kv]

    def add_memory_gradient(layer):
        for k in range(1, DP):
            ag_copy(layer, k).wait_recv()
        for kv in range(2):
            term = lax.dot_general(
                kvg[layer, kv],
                w_v[layer, kv, :, mine],
                (((0,), (0,)), ((), ())),
                preferred_element_type=F32,
            ).reshape(CORES, CHIPS, tokens, quarter)
            if layer == 0 and kv == 0:
                gm_v[...] = term
            else:
                gm_v[...] += term

    for layer in range(layers - 2):
        add_memory_gradient(layer)
    reduce(layers - 1)

    att_out = pltpu.make_async_copy(att_t, att_hbm, out_sem.at[1])
    gq_out = pltpu.make_async_copy(gq_t, gq_hbm, out_sem.at[2])
    att_out.start()
    gq_out.start()
    for layer in range(max(layers - 2, 0), layers):
        add_memory_gradient(layer)
    kvg_out = pltpu.make_async_copy(kvg, kvg_hbm, out_sem.at[3])
    kvg_out.start()
    gm_copy = pltpu.make_async_remote_copy(
        src_ref=gm_v.at[1 - core],
        dst_ref=gm_landed,
        send_sem=gm_sem.at[0],
        recv_sem=gm_sem.at[1],
        device_id=sib,
        device_id_type=MESH,
    )
    gm_copy.start()
    for copy in z_copies + d_copies + s_copies:
        copy.wait_send()
    for layer in range(layers):
        for t in range(DP - 1):
            rs_copy(layer, t).wait_send()
            ag_copy(layer, t + 1).wait_send()
    gm_copy.wait()
    gm_landed[...] += gm_v[core]
    gm_outs = [
        pltpu.make_async_copy(gm_landed.at[(z + k) % CHIPS], hbm, out_sem.at[4 + k])
        for k, hbm in enumerate((gm0_hbm, gm1_hbm, gm2_hbm, gm3_hbm))
    ]
    for copy in gm_outs:
        copy.start()
    for copy in [mem_out, att_out, gq_out, kvg_out] + gm_outs:
        copy.wait()


def attention(queries, memory, w_key, w_value, grad_out):
    layers, rows, width = queries.shape
    tokens, model = memory.shape
    quarter = model // DP
    mem_total = tokens * CHIPS * CORES
    any_spec = pl.BlockSpec(memory_space=pl.ANY)
    dma = pltpu.SemaphoreType.DMA
    out_shape = (
        jax.ShapeDtypeStruct((layers, width, rows), BF16),
        jax.ShapeDtypeStruct((layers, width, rows), BF16),
        jax.ShapeDtypeStruct((layers, 2, width, mem_total), BF16),
        jax.ShapeDtypeStruct((DP, CORES, CHIPS, tokens, quarter), BF16),
    ) + (jax.ShapeDtypeStruct((tokens, quarter), F32),) * CHIPS
    return pl.pallas_call(
        attention_kernel,
        out_shape=out_shape,
        in_specs=[any_spec, pl.BlockSpec(memory_space=pltpu.HBM)] + [any_spec] * 3,
        out_specs=(any_spec,) * (4 + CHIPS),
        scratch_shapes=[
            pltpu.VMEM(queries.shape, BF16),
            pltpu.VMEM(queries.shape, BF16),
            pltpu.VMEM((layers, width, rows), BF16),
            pltpu.VMEM((layers, width, rows), BF16),
            pltpu.VMEM((layers, width, rows), BF16),
            pltpu.VMEM((layers, width, rows), BF16),
            pltpu.VMEM((layers, 2, width, model), BF16),
            pltpu.VMEM(memory.shape, BF16),
            pltpu.VMEM((DP, CORES, CHIPS, tokens, quarter), BF16),
            pltpu.VMEM((DP, quarter, mem_total), BF16),
            pltpu.VMEM((layers, 2, width, mem_total), F32),
            pltpu.VMEM((layers, 2, width, mem_total), BF16),
            pltpu.VMEM((layers, DP - 1, 2, PAIR, mem_total), BF16),
            pltpu.VMEM((layers, 2, PAIR, mem_total), F32),
            pltpu.VMEM((layers, DP - 1, 2, PAIR, mem_total), BF16),
            pltpu.VMEM((layers, 2, width, mem_total), BF16),
            pltpu.VMEM((CORES, CHIPS, tokens, quarter), F32),
            pltpu.VMEM((CHIPS, tokens, quarter), F32),
            dma((3,)),
            dma((DP, 2)),
            dma((4 + CHIPS,)),
            dma((CHIPS - 1,)),
            dma((CHIPS - 1,)),
            dma((DP - 1,)),
            dma((DP - 1,)),
            dma((DP,)),
            dma((DP,)),
            dma((layers, DP - 1)),
            dma((layers, DP - 1)),
            dma((layers, DP - 1)),
            dma((layers, DP - 1)),
            dma((2,)),
        ],
        compiler_params=pltpu.CompilerParams(
            collective_id=0, has_side_effects=True, vmem_limit_bytes=52 * 2**20
        ),
        cost_estimate=pl.CostEstimate(
            flops=8 * 10**9, bytes_accessed=35 * 10**6, transcendentals=2 * 10**6
        ),
        name="attention",
    )(queries, memory, w_key, w_value, grad_out)


def weight_kernel(kvg_ref, mem_ref, turned_ref, out_ref, back_ref):
    out_ref[0] = jnp.dot(
        kvg_ref[0, 0], mem_ref[pl.program_id(1)], preferred_element_type=F32
    )
    back_ref[0] = turned_ref[0].T


def weight_gradient(kvg, mem, turned, kv):
    layers, _, width, mem_total = kvg.shape
    quarter = mem.shape[-1]
    model = DP * quarter
    rows = turned.shape[-1]
    return pl.pallas_call(
        weight_kernel,
        grid=(layers, DP),
        in_specs=[
            pl.BlockSpec((1, 1, width, mem_total), lambda l, j: (l, kv, 0, 0)),
            pl.BlockSpec((DP, mem_total, quarter), lambda l, j: (0, 0, 0)),
            pl.BlockSpec((1, PAIR, rows), lambda l, j: (l, j, 0)),
        ],
        out_specs=[
            pl.BlockSpec((1, width, quarter), lambda l, j: (l, 0, j)),
            pl.BlockSpec((1, rows, PAIR), lambda l, j: (l, 0, j)),
        ],
        out_shape=(
            jax.ShapeDtypeStruct((layers, width, model), F32),
            jax.ShapeDtypeStruct((layers, rows, width), BF16),
        ),
        compiler_params=pltpu.CompilerParams(vmem_limit_bytes=32 * 2**20),
        cost_estimate=pl.CostEstimate(
            flops=2 * layers * width * mem_total * model,
            bytes_accessed=4 * layers * width * (model + rows),
            transcendentals=0,
        ),
        name=("grad_w_key", "grad_w_value")[kv],
    )(kvg, mem, turned)


def place_kernel(*refs):
    out_ref = refs[-1]
    quarter = refs[0].shape[-1]
    i = lax.axis_index("dp")
    for k, ref in enumerate(refs[:-1]):
        j = (i + DP - k) % DP
        out_ref[:, pl.ds(pl.multiple_of(j * quarter, quarter), quarter)] = ref[...]


def fused_shards(queries, memory, w_key, w_value, grad_out):
    attended_t, grad_queries_t, kvg, mem, *gm_parts = attention(
        queries, memory, w_key, w_value, grad_out
    )
    tokens, model = memory.shape
    mem = mem.reshape(DP, tokens * CHIPS * CORES, model // DP)
    gm = gm_parts[0]
    for k in range(1, CHIPS):
        ring = [
            (z * CORES + core, (z + k) % CHIPS * CORES + core)
            for z in range(CHIPS)
            for core in range(CORES)
        ]
        gm = gm + lax.ppermute(gm_parts[k], "mp", ring)
    grad_w_key, attended = weight_gradient(kvg, mem, attended_t, 0)
    grad_w_key, gm = lax.optimization_barrier((grad_w_key, gm))
    quarters = [gm] + [
        lax.ppermute(gm, "dp", [(i, (i + k) % DP) for i in range(DP)]) for k in range(1, DP)
    ]
    grad_w_value, grad_queries = weight_gradient(kvg, mem, grad_queries_t, 1)
    grad_memory = pl.pallas_call(
        place_kernel,
        in_specs=[pl.BlockSpec(memory_space=pltpu.VMEM)] * DP,
        out_specs=pl.BlockSpec(memory_space=pltpu.VMEM),
        out_shape=jax.ShapeDtypeStruct((tokens, model), F32),
        name="place",
    )(*quarters)
    return attended, grad_queries, grad_memory, grad_w_key, grad_w_value


def shards(queries, memory, w_key, w_value, grad_out):
    layers, rows, width = queries.shape
    heads_dev = width // HEAD_WIDTH
    mem_all = lax.all_gather(memory, "mp", axis=0, tiled=True)
    mem_total = mem_all.shape[0]
    keys = jnp.einsum("md,lcd->lmc", mem_all, w_key, preferred_element_type=jnp.float32).astype(
        jnp.bfloat16
    )
    values = jnp.einsum("md,lcd->lmc", mem_all, w_value, preferred_element_type=jnp.float32).astype(
        jnp.bfloat16
    )
    per_head_queries = queries.reshape(layers, rows, heads_dev, HEAD_WIDTH)
    per_head_keys = keys.reshape(layers, mem_total, heads_dev, HEAD_WIDTH)
    per_head_values = values.reshape(layers, mem_total, heads_dev, HEAD_WIDTH)
    head_output_gradient = grad_out.reshape(layers, rows, heads_dev, HEAD_WIDTH)
    attention_logits = jnp.einsum(
        "lrhd,lmhd->lhrm", per_head_queries, per_head_keys, preferred_element_type=jnp.float32
    )
    row_max = jnp.max(attention_logits, axis=-1, keepdims=True)
    exp_scores = jnp.exp(attention_logits - row_max)
    attn_probs = exp_scores / jnp.sum(exp_scores, axis=-1, keepdims=True)
    batch_probabilities = attn_probs.astype(jnp.bfloat16)
    attended = (
        jnp.einsum(
            "lhrm,lmhd->lrhd",
            batch_probabilities,
            per_head_values,
            preferred_element_type=jnp.float32,
        )
        .reshape(layers, rows, width)
        .astype(jnp.bfloat16)
    )
    probability_gradient = jnp.einsum(
        "lrhd,lmhd->lhrm", head_output_gradient, per_head_values, preferred_element_type=jnp.float32
    )
    row_delta = jnp.sum(attn_probs * probability_gradient, axis=-1, keepdims=True)
    logit_gradient = (attn_probs * (probability_gradient - row_delta)).astype(jnp.bfloat16)
    grad_queries = (
        jnp.einsum(
            "lhrm,lmhd->lrhd", logit_gradient, per_head_keys, preferred_element_type=jnp.float32
        )
        .reshape(layers, rows, width)
        .astype(jnp.bfloat16)
    )
    key_part = jnp.einsum(
        "lhrm,lrhd->lmhd", logit_gradient, per_head_queries, preferred_element_type=jnp.float32
    ).reshape(layers, mem_total, width)
    value_part = jnp.einsum(
        "lhrm,lrhd->lmhd",
        batch_probabilities,
        head_output_gradient,
        preferred_element_type=jnp.float32,
    ).reshape(layers, mem_total, width)
    key_sum, value_sum = lax.psum((key_part, value_part), "dp")
    key_gradient = key_sum.astype(jnp.bfloat16)
    value_gradient = value_sum.astype(jnp.bfloat16)
    grad_w_key = jnp.einsum(
        "lmc,md->lcd", key_gradient, mem_all, preferred_element_type=jnp.float32
    )
    grad_w_value = jnp.einsum(
        "lmc,md->lcd", value_gradient, mem_all, preferred_element_type=jnp.float32
    )
    grad_memory = lax.psum_scatter(
        jnp.einsum("lmc,lcd->md", key_gradient, w_key, preferred_element_type=jnp.float32)
        + jnp.einsum("lmc,lcd->md", value_gradient, w_value, preferred_element_type=jnp.float32),
        "mp",
        scatter_dimension=0,
        tiled=True,
    )
    return (attended, grad_queries, grad_memory, grad_w_key, grad_w_value)


def solution(mesh):
    def choose(queries, memory, w_key, w_value, grad_out):
        fits = (
            mesh.shape["dp"] == DP
            and mesh.shape["mp"] == CHIPS * CORES
            and queries.shape[2] == DP * PAIR
            and queries.shape[1] % (128 * DP) == 0
            and memory.shape[0] == PAIR // (CHIPS * CORES)
            and memory.shape[1] % (DP * 128) == 0
        )
        run = fused_shards if fits else shards
        return run(queries, memory, w_key, w_value, grad_out)

    return jax.shard_map(
        choose,
        mesh=mesh,
        in_specs=(
            P(None, "dp", "mp"),
            P("mp", None),
            P(None, "mp", None),
            P(None, "mp", None),
            P(None, "dp", "mp"),
        ),
        out_specs=(
            P(None, "dp", "mp"),
            P(None, "dp", "mp"),
            P("mp", None),
            P(None, "mp", None),
            P(None, "mp", None),
        ),
        check_vma=False,
    )
```

```python
import functools

import jax
import jax.numpy as jnp
from jax import lax
from jax.experimental import pallas as pl
from jax.experimental.pallas import tpu as pltpu
from jax.sharding import PartitionSpec as P

HEAD_WIDTH = 64
PAIR = 2 * HEAD_WIDTH
MESH = pl.DeviceIdType.MESH
F32 = jnp.float32
BF16 = jnp.bfloat16

DP, CHIPS, CORES = 4, 4, 2


def attention_kernel(
    q_hbm, mem_in, wk_hbm, wv_hbm, g_hbm,
    att_hbm, gq_hbm, kvg_hbm, mem_hbm, gm0_hbm, gm1_hbm, gm2_hbm, gm3_hbm,
    q_v, g_v, qt_v, gt_v, att_t, gq_t, w_v, mem_ref, mg, mt, acc, kvt, part, own, hold, landed, kvg,
    gm_v, gm_landed,
    in_sem, w_sem, out_sem, z_send, z_recv, d_send, d_recv, s_send, s_recv,
    rs_send, rs_recv, ag_send, ag_recv, gm_sem,
):
    layers, rows, width = q_v.shape
    tokens = mem_ref.shape[0]
    quarter = mem_ref.shape[1] // DP
    mem_total = tokens * CHIPS * CORES
    i = lax.axis_index("dp")
    me = lax.axis_index("mp")
    z = me // CORES
    core = me % CORES
    sibling = z * CORES + 1 - core

    def z_peer(k):
        return {"dp": i, "mp": ((z + k) % CHIPS) * CORES + core}

    x, y = i % 2, i // 2
    i_x, i_y, i_far = y * 2 + 1 - x, (1 - y) * 2 + x, DP - 1 - i
    order = (i, i_x, i_y, i_far)
    to_x, to_y = {"dp": i_x, "mp": me}, {"dp": i_y, "mp": me}

    sib = {"dp": i, "mp": sibling}

    def columns(step):
        return pl.ds(pl.multiple_of(order[step] * quarter, quarter), quarter)

    def load_w(step):
        cols = columns(step)
        return [
            pltpu.make_async_copy(
                hbm.at[:, :, cols], w_v.at[:, kv, :, cols], w_sem.at[step, kv]
            )
            for kv, hbm in enumerate((wk_hbm, wv_hbm))
        ]

    load_mem = pltpu.make_async_copy(mem_in, mem_ref, in_sem.at[2])
    load_q = pltpu.make_async_copy(q_hbm, q_v, in_sem.at[0])
    load_g = pltpu.make_async_copy(g_hbm, g_v, in_sem.at[1])
    load_mem.start()
    load_q.start()
    load_g.start()
    for step in range(DP):
        for copy in load_w(step):
            copy.start()

    barrier = pltpu.get_barrier_semaphore()
    for k in range(1, CHIPS):
        pl.semaphore_signal(barrier, inc=1, device_id=z_peer(k), device_id_type=MESH)
    for peer in (to_x, to_y, sib):
        pl.semaphore_signal(barrier, inc=1, device_id=peer, device_id_type=MESH)
    load_mem.wait()
    pl.semaphore_wait(barrier, CHIPS - 1 + 3)

    mine = columns(0)
    z_copies = []
    for k in range(1, CHIPS):
        z_copies.append(
            pltpu.make_async_remote_copy(
                src_ref=mem_ref.at[:, mine],
                dst_ref=mg.at[i, core, z],
                send_sem=z_send.at[k - 1],
                recv_sem=z_recv.at[k - 1],
                device_id=z_peer(k),
                device_id_type=MESH,
            )
        )
        z_copies[-1].start()
    mg[i, core, z] = mem_ref[:, mine]
    for copy in z_copies:
        copy.wait_recv()

    def to_sibling(step):
        block = mg.at[order[step], core]
        return pltpu.make_async_remote_copy(
            src_ref=block,
            dst_ref=block,
            send_sem=s_send.at[step],
            recv_sem=s_recv.at[step],
            device_id=sib,
            device_id_type=MESH,
        )

    def gather_copy(block, at, peer):
        return pltpu.make_async_remote_copy(
            src_ref=block,
            dst_ref=block,
            send_sem=d_send.at[at],
            recv_sem=d_recv.at[at],
            device_id=peer,
            device_id_type=MESH,
        )

    half = CHIPS // 2
    s_copies = [to_sibling(step) for step in range(DP)]
    d_copies = [
        gather_copy(mg.at[i, core], 0, to_x),
        gather_copy(mg.at[i, core], 1, to_y),
        gather_copy(mg.at[i_x, core, pl.ds(0, half)], 2, to_y),
        gather_copy(mg.at[i_y, core, pl.ds(half, half)], 3, to_x),
    ]
    d_copies[0].start()
    d_copies[1].start()
    s_copies[0].start()

    def pair_rows(pair):
        return pl.ds(pl.multiple_of(pair * PAIR, PAIR), PAIR)

    load_q.wait()
    load_g.wait()

    @pl.loop(0, layers * DP)
    def turn(n):
        lanes = pair_rows(n % DP)
        qt_v[n // DP, lanes, :] = q_v[n // DP, :, lanes].T
        gt_v[n // DP, lanes, :] = g_v[n // DP, :, lanes].T

    def project(layer, kv, step):
        return jnp.dot(w_v[layer, kv, :, columns(step)], mt[step], preferred_element_type=F32)

    for step in range(DP):
        if step == 1:
            for near in range(2):
                d_copies[near].wait_recv()
                d_copies[2 + near].start()
                s_copies[1 + near].start()
        elif step == 3:
            d_copies[2].wait_recv()
            d_copies[3].wait_recv()
            s_copies[3].start()
        for copy in load_w(step):
            copy.wait()
        s_copies[step].wait_recv()
        mt[step] = mg[order[step]].reshape(mem_total, quarter).T
        if step == 0:

            @pl.loop(0, layers * 2)
            def first_quarter(n):
                acc[n // 2, n % 2] = project(n // 2, n % 2, 0)

        elif step < DP - 1:

            @pl.loop(0, 2)
            def layer_0(kv):
                acc[0, kv] += project(0, kv, step)

        else:

            @pl.loop(0, 2)
            def layer_0_last(kv):
                kvt[0, kv] = (acc[0, kv] + project(0, kv, step)).astype(BF16)

    def finish_projection(layer):
        @pl.loop(0, 2)
        def one(kv):
            total = acc[layer, kv]
            for step in range(1, DP):
                total = total + project(layer, kv, step)
            kvt[layer, kv] = total.astype(BF16)

    mem_out = pltpu.make_async_copy(mg, mem_hbm, out_sem.at[0])
    mem_out.start()

    def rs_copy(layer, slot):
        return pltpu.make_async_remote_copy(
            src_ref=part.at[layer, slot],
            dst_ref=landed.at[layer, slot],
            send_sem=rs_send.at[layer, slot],
            recv_sem=rs_recv.at[layer, slot],
            device_id=to_x if slot % 2 == 0 else to_y,
            device_id_type=MESH,
        )

    def send_part(layer, slot, term):
        part[layer, slot] = term.astype(BF16)
        rs_copy(layer, slot).start()

    def came(layer, slot):
        rs_copy(layer, slot).wait_recv()
        return landed[layer, slot].astype(F32)

    def ag_copy(layer, at):
        block = (
            kvg.at[layer, :, pair_rows(i), :],
            kvg.at[layer, :, pair_rows(i), :],
            kvg.at[layer, 0, pair_rows(i_x), :],
            kvg.at[layer, 1, pair_rows(i_y), :],
        )[at]
        return pltpu.make_async_remote_copy(
            src_ref=block,
            dst_ref=block,
            send_sem=ag_send.at[layer, at],
            recv_sem=ag_recv.at[layer, at],
            device_id=(to_x, to_y, to_y, to_x)[at],
            device_id_type=MESH,
        )

    def reduce(layer):
        keys = own[layer, 0] + came(layer, 2) + came(layer, 5)
        values = own[layer, 1] + came(layer, 3) + came(layer, 4)
        kvg[layer, 0, pair_rows(i), :] = keys.astype(BF16)
        kvg[layer, 1, pair_rows(i), :] = values.astype(BF16)
        ag_copy(layer, 0).start()
        ag_copy(layer, 1).start()

    def pass_on(layer):
        for near in range(2):
            ag_copy(layer, near).wait_recv()
            ag_copy(layer, 2 + near).start()

    def head_masks(axis):
        return lax.broadcasted_iota(jnp.int32, (PAIR, PAIR), axis) < HEAD_WIDTH

    first_row, first_lane = head_masks(0), head_masks(1)

    def split_heads(block, mask, axis):
        zero = jnp.zeros_like(block)
        return jnp.concatenate(
            [jnp.where(mask, block, zero), jnp.where(mask, zero, block)], axis=axis
        )

    def own_blocks(both):
        return jnp.where(first_row, both[:, :mem_total], both[:, mem_total:])

    def dot_nt(lhs, rhs):
        return lax.dot_general(lhs, rhs, (((1,), (1,)), ((), ())), preferred_element_type=F32)

    def attend(layer, pair):
        lanes = pair_rows(pair)
        queries, grads = qt_v[layer, lanes, :], gt_v[layer, lanes, :]
        keys, values = kvt[layer, 0, lanes, :], kvt[layer, 1, lanes, :]
        scores = jnp.dot(
            split_heads(keys.T, first_lane, 0), queries, preferred_element_type=F32
        )
        grad_probs = jnp.dot(
            split_heads(values.T, first_lane, 0), grads, preferred_element_type=F32
        )
        probs_b, grad_scores = [], []
        for head in range(2):
            probs_row, grads_row = [], []
            for chunk in range(rows // 128):
                at = (
                    slice(head * mem_total, (head + 1) * mem_total),
                    slice(chunk * 128, (chunk + 1) * 128),
                )
                s, gp = scores[at], grad_probs[at]
                e = jnp.exp(s - jnp.max(s, axis=0, keepdims=True))
                scale = 1.0 / jnp.sum(e, axis=0, keepdims=True)
                delta = jnp.sum(e * gp, axis=0, keepdims=True) * scale
                probs = e * scale
                probs_row.append(probs.astype(BF16))
                grads_row.append((probs * (gp - delta)).astype(BF16))
            probs_b.append(jnp.concatenate(probs_row, axis=1))
            grad_scores.append(jnp.concatenate(grads_row, axis=1))
        probs_b = jnp.concatenate(probs_b, axis=0)
        grad_scores = jnp.concatenate(grad_scores, axis=0)
        att_t[layer, lanes, :] = jnp.dot(
            split_heads(values, first_row, 1), probs_b, preferred_element_type=F32
        ).astype(BF16)
        gq_t[layer, lanes, :] = jnp.dot(
            split_heads(keys, first_row, 1), grad_scores, preferred_element_type=F32
        ).astype(BF16)
        return own_blocks(dot_nt(queries, grad_scores)), own_blocks(dot_nt(grads, probs_b))

    @pl.loop(0, layers)
    def one_layer(layer):
        @pl.when(layer >= 1)
        def _():
            finish_projection(layer)
            reduce(layer - 1)

        far, by_x = attend(layer, i_far), attend(layer, i_x)
        send_part(layer, 0, far[0])
        send_part(layer, 1, far[1])
        send_part(layer, 2, by_x[0])
        hold[0] = by_x[1]
        by_y, mine_both = attend(layer, i_y), attend(layer, i)
        send_part(layer, 3, by_y[1])
        hold[1] = by_y[0]
        for kv in range(2):
            own[layer, kv] = mine_both[kv]
        send_part(layer, 4, hold[0] + came(layer, 1))
        send_part(layer, 5, hold[1] + came(layer, 0))

        @pl.when(layer >= 1)
        def _():
            pass_on(layer - 1)

    def add_memory_gradient(layer):
        for at in (2, 3):
            ag_copy(layer, at).wait_recv()
        for kv in range(2):
            term = lax.dot_general(
                kvg[layer, kv],
                w_v[layer, kv, :, mine],
                (((0,), (0,)), ((), ())),
                preferred_element_type=F32,
            ).reshape(CORES, CHIPS, tokens, quarter)
            if layer == 0 and kv == 0:
                gm_v[...] = term
            else:
                gm_v[...] += term

    reduce(layers - 1)

    att_out = pltpu.make_async_copy(att_t, att_hbm, out_sem.at[1])
    gq_out = pltpu.make_async_copy(gq_t, gq_hbm, out_sem.at[2])
    att_out.start()
    gq_out.start()
    for layer in range(layers):
        if layer == layers - 1:
            pass_on(layer)
        add_memory_gradient(layer)
    kvg_out = pltpu.make_async_copy(kvg, kvg_hbm, out_sem.at[3])
    kvg_out.start()
    gm_copy = pltpu.make_async_remote_copy(
        src_ref=gm_v.at[1 - core],
        dst_ref=gm_landed,
        send_sem=gm_sem.at[0],
        recv_sem=gm_sem.at[1],
        device_id=sib,
        device_id_type=MESH,
    )
    gm_copy.start()
    for copy in z_copies + d_copies + s_copies:
        copy.wait_send()
    for layer in range(layers):
        for slot in range(6):
            rs_copy(layer, slot).wait_send()
        for at in range(4):
            ag_copy(layer, at).wait_send()
    gm_copy.wait()
    gm_landed[...] += gm_v[core]
    gm_outs = [
        pltpu.make_async_copy(gm_landed.at[(z + k) % CHIPS], hbm, out_sem.at[4 + k])
        for k, hbm in enumerate((gm0_hbm, gm1_hbm, gm2_hbm, gm3_hbm))
    ]
    for copy in gm_outs:
        copy.start()
    for copy in [mem_out, att_out, gq_out, kvg_out] + gm_outs:
        copy.wait()


def attention(queries, memory, w_key, w_value, grad_out):
    layers, rows, width = queries.shape
    tokens, model = memory.shape
    quarter = model // DP
    mem_total = tokens * CHIPS * CORES
    any_spec = pl.BlockSpec(memory_space=pl.ANY)
    dma = pltpu.SemaphoreType.DMA
    out_shape = (
        jax.ShapeDtypeStruct((layers, width, rows), BF16),
        jax.ShapeDtypeStruct((layers, width, rows), BF16),
        jax.ShapeDtypeStruct((layers, 2, width, mem_total), BF16),
        jax.ShapeDtypeStruct((DP, CORES, CHIPS, tokens, quarter), BF16),
    ) + (jax.ShapeDtypeStruct((tokens, quarter), F32),) * CHIPS
    return pl.pallas_call(
        attention_kernel,
        out_shape=out_shape,
        in_specs=[any_spec, pl.BlockSpec(memory_space=pltpu.HBM)] + [any_spec] * 3,
        out_specs=(any_spec,) * (4 + CHIPS),
        scratch_shapes=[
            pltpu.VMEM(queries.shape, BF16),
            pltpu.VMEM(queries.shape, BF16),
            pltpu.VMEM((layers, width, rows), BF16),
            pltpu.VMEM((layers, width, rows), BF16),
            pltpu.VMEM((layers, width, rows), BF16),
            pltpu.VMEM((layers, width, rows), BF16),
            pltpu.VMEM((layers, 2, width, model), BF16),
            pltpu.VMEM(memory.shape, BF16),
            pltpu.VMEM((DP, CORES, CHIPS, tokens, quarter), BF16),
            pltpu.VMEM((DP, quarter, mem_total), BF16),
            pltpu.VMEM((layers, 2, width, mem_total), F32),
            pltpu.VMEM((layers, 2, width, mem_total), BF16),
            pltpu.VMEM((layers, 6, PAIR, mem_total), BF16),
            pltpu.VMEM((layers, 2, PAIR, mem_total), F32),
            pltpu.VMEM((2, PAIR, mem_total), F32),
            pltpu.VMEM((layers, 6, PAIR, mem_total), BF16),
            pltpu.VMEM((layers, 2, width, mem_total), BF16),
            pltpu.VMEM((CORES, CHIPS, tokens, quarter), F32),
            pltpu.VMEM((CHIPS, tokens, quarter), F32),
            dma((3,)),
            dma((DP, 2)),
            dma((4 + CHIPS,)),
            dma((CHIPS - 1,)),
            dma((CHIPS - 1,)),
            dma((4,)),
            dma((4,)),
            dma((DP,)),
            dma((DP,)),
            dma((layers, 6)),
            dma((layers, 6)),
            dma((layers, 4)),
            dma((layers, 4)),
            dma((2,)),
        ],
        compiler_params=pltpu.CompilerParams(
            collective_id=0, has_side_effects=True, vmem_limit_bytes=60 * 2**20
        ),
        cost_estimate=pl.CostEstimate(
            flops=8 * 10**9, bytes_accessed=35 * 10**6, transcendentals=2 * 10**6
        ),
        name="attention",
    )(queries, memory, w_key, w_value, grad_out)


def weight_kernel(
    kv, kvg_hbm, mem_hbm, turned_hbm, out_hbm, back_hbm,
    kvg_v, mem_v, turned_v, ring, back_v, in_sem, ring_sem, back_sem,
):
    layers, width, _ = kvg_v.shape
    quarter = mem_v.shape[-1]
    slots = ring.shape[0]
    loads = [
        pltpu.make_async_copy(kvg_hbm.at[:, kv], kvg_v, in_sem.at[0]),
        pltpu.make_async_copy(mem_hbm, mem_v, in_sem.at[1]),
        pltpu.make_async_copy(turned_hbm, turned_v, in_sem.at[2]),
    ]
    for copy in loads:
        copy.start()
    loads[0].wait()
    loads[1].wait()

    def write(n):
        at = pl.ds(pl.multiple_of(n % DP * PAIR, PAIR), PAIR)
        return pltpu.make_async_copy(
            ring.at[n % slots], out_hbm.at[n // DP, at, :], ring_sem.at[n % slots]
        )

    def write_back(layer):
        return pltpu.make_async_copy(back_v.at[layer], back_hbm.at[layer], back_sem.at[layer])

    @pl.loop(0, layers * DP)
    def step(n):
        layer = n // DP
        at = pl.ds(pl.multiple_of(n % DP * PAIR, PAIR), PAIR)

        @pl.when(n >= slots)
        def _():
            write(n - slots).wait()

        for j in range(DP):
            ring[n % slots, :, j * quarter : (j + 1) * quarter] = jnp.dot(
                kvg_v[layer, at, :], mem_v[j], preferred_element_type=F32
            )
        write(n).start()

        @pl.when(n == 0)
        def _():
            loads[2].wait()

        back_v[layer, :, at] = turned_v[layer, at, :].T

        @pl.when(n % DP == DP - 1)
        def _():
            write_back(layer).start()

    for n in range(layers * DP - slots, layers * DP):
        write(n).wait()
    for layer in range(layers):
        write_back(layer).wait()


def weight_gradient(kvg, mem, turned, kv):
    layers, _, width, mem_total = kvg.shape
    quarter = mem.shape[-1]
    model = DP * quarter
    rows = turned.shape[-1]
    slots = 4
    any_spec = pl.BlockSpec(memory_space=pl.ANY)
    dma = pltpu.SemaphoreType.DMA
    return pl.pallas_call(
        functools.partial(weight_kernel, kv),
        in_specs=[any_spec] * 3,
        out_specs=[any_spec] * 2,
        out_shape=(
            jax.ShapeDtypeStruct((layers, width, model), F32),
            jax.ShapeDtypeStruct((layers, rows, width), BF16),
        ),
        scratch_shapes=[
            pltpu.VMEM((layers, width, mem_total), BF16),
            pltpu.VMEM(mem.shape, BF16),
            pltpu.VMEM(turned.shape, BF16),
            pltpu.VMEM((slots, PAIR, model), F32),
            pltpu.VMEM((layers, rows, width), BF16),
            dma((3,)),
            dma((slots,)),
            dma((layers,)),
        ],
        compiler_params=pltpu.CompilerParams(vmem_limit_bytes=60 * 2**20),
        cost_estimate=pl.CostEstimate(
            flops=2 * layers * width * mem_total * model,
            bytes_accessed=4 * layers * width * (model + rows),
            transcendentals=0,
        ),
        name=("grad_w_key", "grad_w_value")[kv],
    )(kvg, mem, turned)


def place_kernel(*refs):
    out_ref = refs[-1]
    quarter = refs[0].shape[-1]
    i = lax.axis_index("dp")
    for k, ref in enumerate(refs[:-1]):
        j = (i + DP - k) % DP
        out_ref[:, pl.ds(pl.multiple_of(j * quarter, quarter), quarter)] = ref[...]


def fused_shards(queries, memory, w_key, w_value, grad_out):
    attended_t, grad_queries_t, kvg, mem, *gm_parts = attention(
        queries, memory, w_key, w_value, grad_out
    )
    tokens, model = memory.shape
    mem = mem.reshape(DP, tokens * CHIPS * CORES, model // DP)
    gm = gm_parts[0]
    for k in range(1, CHIPS):
        ring = [
            (z * CORES + core, (z + k) % CHIPS * CORES + core)
            for z in range(CHIPS)
            for core in range(CORES)
        ]
        gm = gm + lax.ppermute(gm_parts[k], "mp", ring)
    grad_w_key, attended = weight_gradient(kvg, mem, attended_t, 0)
    grad_w_key, gm = lax.optimization_barrier((grad_w_key, gm))
    quarters = [gm] + [
        lax.ppermute(gm, "dp", [(i, (i + k) % DP) for i in range(DP)]) for k in range(1, DP)
    ]
    grad_w_value, grad_queries = weight_gradient(kvg, mem, grad_queries_t, 1)
    grad_memory = pl.pallas_call(
        place_kernel,
        in_specs=[pl.BlockSpec(memory_space=pltpu.VMEM)] * DP,
        out_specs=pl.BlockSpec(memory_space=pltpu.VMEM),
        out_shape=jax.ShapeDtypeStruct((tokens, model), F32),
        name="place",
    )(*quarters)
    return attended, grad_queries, grad_memory, grad_w_key, grad_w_value


def shards(queries, memory, w_key, w_value, grad_out):
    layers, rows, width = queries.shape
    heads_dev = width // HEAD_WIDTH
    mem_all = lax.all_gather(memory, "mp", axis=0, tiled=True)
    mem_total = mem_all.shape[0]
    keys = jnp.einsum("md,lcd->lmc", mem_all, w_key, preferred_element_type=jnp.float32).astype(
        jnp.bfloat16
    )
    values = jnp.einsum("md,lcd->lmc", mem_all, w_value, preferred_element_type=jnp.float32).astype(
        jnp.bfloat16
    )
    per_head_queries = queries.reshape(layers, rows, heads_dev, HEAD_WIDTH)
    per_head_keys = keys.reshape(layers, mem_total, heads_dev, HEAD_WIDTH)
    per_head_values = values.reshape(layers, mem_total, heads_dev, HEAD_WIDTH)
    head_output_gradient = grad_out.reshape(layers, rows, heads_dev, HEAD_WIDTH)
    attention_logits = jnp.einsum(
        "lrhd,lmhd->lhrm", per_head_queries, per_head_keys, preferred_element_type=jnp.float32
    )
    row_max = jnp.max(attention_logits, axis=-1, keepdims=True)
    exp_scores = jnp.exp(attention_logits - row_max)
    attn_probs = exp_scores / jnp.sum(exp_scores, axis=-1, keepdims=True)
    batch_probabilities = attn_probs.astype(jnp.bfloat16)
    attended = (
        jnp.einsum(
            "lhrm,lmhd->lrhd",
            batch_probabilities,
            per_head_values,
            preferred_element_type=jnp.float32,
        )
        .reshape(layers, rows, width)
        .astype(jnp.bfloat16)
    )
    probability_gradient = jnp.einsum(
        "lrhd,lmhd->lhrm", head_output_gradient, per_head_values, preferred_element_type=jnp.float32
    )
    row_delta = jnp.sum(attn_probs * probability_gradient, axis=-1, keepdims=True)
    logit_gradient = (attn_probs * (probability_gradient - row_delta)).astype(jnp.bfloat16)
    grad_queries = (
        jnp.einsum(
            "lhrm,lmhd->lrhd", logit_gradient, per_head_keys, preferred_element_type=jnp.float32
        )
        .reshape(layers, rows, width)
        .astype(jnp.bfloat16)
    )
    key_part = jnp.einsum(
        "lhrm,lrhd->lmhd", logit_gradient, per_head_queries, preferred_element_type=jnp.float32
    ).reshape(layers, mem_total, width)
    value_part = jnp.einsum(
        "lhrm,lrhd->lmhd",
        batch_probabilities,
        head_output_gradient,
        preferred_element_type=jnp.float32,
    ).reshape(layers, mem_total, width)
    key_sum, value_sum = lax.psum((key_part, value_part), "dp")
    key_gradient = key_sum.astype(jnp.bfloat16)
    value_gradient = value_sum.astype(jnp.bfloat16)
    grad_w_key = jnp.einsum(
        "lmc,md->lcd", key_gradient, mem_all, preferred_element_type=jnp.float32
    )
    grad_w_value = jnp.einsum(
        "lmc,md->lcd", value_gradient, mem_all, preferred_element_type=jnp.float32
    )
    grad_memory = lax.psum_scatter(
        jnp.einsum("lmc,lcd->md", key_gradient, w_key, preferred_element_type=jnp.float32)
        + jnp.einsum("lmc,lcd->md", value_gradient, w_value, preferred_element_type=jnp.float32),
        "mp",
        scatter_dimension=0,
        tiled=True,
    )
    return (attended, grad_queries, grad_memory, grad_w_key, grad_w_value)


def solution(mesh):
    def choose(queries, memory, w_key, w_value, grad_out):
        fits = (
            mesh.shape["dp"] == DP
            and mesh.shape["mp"] == CHIPS * CORES
            and queries.shape[2] == DP * PAIR
            and queries.shape[1] % (128 * DP) == 0
            and memory.shape[0] == PAIR // (CHIPS * CORES)
            and memory.shape[1] % (DP * 128) == 0
        )
        run = fused_shards if fits else shards
        return run(queries, memory, w_key, w_value, grad_out)

    return jax.shard_map(
        choose,
        mesh=mesh,
        in_specs=(
            P(None, "dp", "mp"),
            P("mp", None),
            P(None, "mp", None),
            P(None, "mp", None),
            P(None, "dp", "mp"),
        ),
        out_specs=(
            P(None, "dp", "mp"),
            P(None, "dp", "mp"),
            P("mp", None),
            P(None, "mp", None),
            P(None, "mp", None),
        ),
        check_vma=False,
    )
```

```python
import functools

import jax
import jax.numpy as jnp
from jax import lax
from jax.experimental import pallas as pl
from jax.experimental.pallas import tpu as pltpu
from jax.sharding import PartitionSpec as P

HEAD_WIDTH = 64
PAIR = 2 * HEAD_WIDTH
MESH = pl.DeviceIdType.MESH
F32 = jnp.float32
BF16 = jnp.bfloat16

DP, CHIPS, CORES = 4, 4, 2


def attention_kernel(
    q_hbm, mem_in, wk_hbm, wv_hbm, g_hbm,
    att_hbm, gq_hbm, kvg_hbm, mem_hbm, gm0_hbm, gm1_hbm, gm2_hbm, gm3_hbm,
    q_v, g_v, qt_v, gt_v, att_t, gq_t, w_v, mem_ref, mg, mt, acc, kvt, part, own, hold, landed, kvg,
    gm_v, gm_landed,
    in_sem, w_sem, out_sem, z_send, z_recv, d_send, d_recv, s_send, s_recv,
    rs_send, rs_recv, ag_send, ag_recv, gm_sem,
):
    layers, rows, width = q_v.shape
    tokens = mem_ref.shape[0]
    quarter = mem_ref.shape[1] // DP
    mem_total = tokens * CHIPS * CORES
    i = lax.axis_index("dp")
    me = lax.axis_index("mp")
    z = me // CORES
    core = me % CORES
    sibling = z * CORES + 1 - core

    def z_peer(k):
        return {"dp": i, "mp": ((z + k) % CHIPS) * CORES + core}

    x, y = i % 2, i // 2
    i_x, i_y, i_far = y * 2 + 1 - x, (1 - y) * 2 + x, DP - 1 - i
    order = (i, i_x, i_y, i_far)
    to_x, to_y, to_far = ({"dp": j, "mp": me} for j in (i_x, i_y, i_far))

    sib = {"dp": i, "mp": sibling}

    def columns(step):
        return pl.ds(pl.multiple_of(order[step] * quarter, quarter), quarter)

    def load_w(step):
        cols = columns(step)
        return [
            pltpu.make_async_copy(
                hbm.at[:, :, cols], w_v.at[:, kv, :, cols], w_sem.at[step, kv]
            )
            for kv, hbm in enumerate((wk_hbm, wv_hbm))
        ]

    load_mem = pltpu.make_async_copy(mem_in, mem_ref, in_sem.at[2])
    load_q = pltpu.make_async_copy(q_hbm, q_v, in_sem.at[0])
    load_g = pltpu.make_async_copy(g_hbm, g_v, in_sem.at[1])
    load_mem.start()
    load_q.start()
    load_g.start()
    for step in range(DP):
        for copy in load_w(step):
            copy.start()

    barrier = pltpu.get_barrier_semaphore()
    for k in range(1, CHIPS):
        pl.semaphore_signal(barrier, inc=1, device_id=z_peer(k), device_id_type=MESH)
    for peer in (to_x, to_y, to_far, sib):
        pl.semaphore_signal(barrier, inc=1, device_id=peer, device_id_type=MESH)
    load_mem.wait()
    pl.semaphore_wait(barrier, CHIPS - 1 + 4)

    mine = columns(0)
    z_copies = []
    for k in range(1, CHIPS):
        z_copies.append(
            pltpu.make_async_remote_copy(
                src_ref=mem_ref.at[:, mine],
                dst_ref=mg.at[i, core, z],
                send_sem=z_send.at[k - 1],
                recv_sem=z_recv.at[k - 1],
                device_id=z_peer(k),
                device_id_type=MESH,
            )
        )
        z_copies[-1].start()
    mg[i, core, z] = mem_ref[:, mine]
    for copy in z_copies:
        copy.wait_recv()

    def to_sibling(step):
        block = mg.at[order[step], core]
        return pltpu.make_async_remote_copy(
            src_ref=block,
            dst_ref=block,
            send_sem=s_send.at[step],
            recv_sem=s_recv.at[step],
            device_id=sib,
            device_id_type=MESH,
        )

    def gather_copy(block, at, peer):
        return pltpu.make_async_remote_copy(
            src_ref=block,
            dst_ref=block,
            send_sem=d_send.at[at],
            recv_sem=d_recv.at[at],
            device_id=peer,
            device_id_type=MESH,
        )

    half = CHIPS // 2
    s_copies = [to_sibling(step) for step in range(DP)]
    d_copies = [
        gather_copy(mg.at[i, core], 0, to_x),
        gather_copy(mg.at[i, core], 1, to_y),
        gather_copy(mg.at[i_x, core, pl.ds(0, half)], 2, to_y),
        gather_copy(mg.at[i_y, core, pl.ds(half, half)], 3, to_x),
    ]
    d_copies[0].start()
    d_copies[1].start()
    s_copies[0].start()

    def pair_rows(pair):
        return pl.ds(pl.multiple_of(pair * PAIR, PAIR), PAIR)

    load_q.wait()
    load_g.wait()

    @pl.loop(0, layers * DP)
    def turn(n):
        lanes = pair_rows(n % DP)
        qt_v[n // DP, lanes, :] = q_v[n // DP, :, lanes].T
        gt_v[n // DP, lanes, :] = g_v[n // DP, :, lanes].T

    def project(layer, kv, step):
        return jnp.dot(w_v[layer, kv, :, columns(step)], mt[step], preferred_element_type=F32)

    for step in range(DP):
        if step == 1:
            for near in range(2):
                d_copies[near].wait_recv()
                d_copies[2 + near].start()
                s_copies[1 + near].start()
        elif step == 3:
            d_copies[2].wait_recv()
            d_copies[3].wait_recv()
            s_copies[3].start()
        for copy in load_w(step):
            copy.wait()
        s_copies[step].wait_recv()
        mt[step] = mg[order[step]].reshape(mem_total, quarter).T
        if step == 0:

            @pl.loop(0, layers * 2)
            def first_quarter(n):
                acc[n // 2, n % 2] = project(n // 2, n % 2, 0)

        elif step < DP - 1:

            @pl.loop(0, 2)
            def layer_0(kv):
                acc[0, kv] += project(0, kv, step)

        else:

            @pl.loop(0, 2)
            def layer_0_last(kv):
                kvt[0, kv] = (acc[0, kv] + project(0, kv, step)).astype(BF16)

    def finish_projection(layer):
        @pl.loop(0, 2)
        def one(kv):
            total = acc[layer, kv]
            for step in range(1, DP):
                total = total + project(layer, kv, step)
            kvt[layer, kv] = total.astype(BF16)

    mem_out = pltpu.make_async_copy(mg, mem_hbm, out_sem.at[0])
    mem_out.start()

    def rs_copy(layer, slot):
        return pltpu.make_async_remote_copy(
            src_ref=part.at[layer, slot],
            dst_ref=landed.at[layer, slot],
            send_sem=rs_send.at[layer, slot],
            recv_sem=rs_recv.at[layer, slot],
            device_id=to_x if slot % 2 == 0 else to_y,
            device_id_type=MESH,
        )

    def send_part(layer, slot, term):
        part[layer, slot] = term.astype(BF16)
        rs_copy(layer, slot).start()

    def came(layer, slot):
        rs_copy(layer, slot).wait_recv()
        return landed[layer, slot].astype(F32)

    def ag_copy(layer, at):
        block = kvg.at[layer, :, pair_rows(i), :]
        return pltpu.make_async_remote_copy(
            src_ref=block,
            dst_ref=block,
            send_sem=ag_send.at[layer, at],
            recv_sem=ag_recv.at[layer, at],
            device_id=(to_far, to_x, to_y)[at],
            device_id_type=MESH,
        )

    def reduce(layer):
        keys = own[layer, 0] + came(layer, 2) + came(layer, 5)
        values = own[layer, 1] + came(layer, 3) + came(layer, 4)
        kvg[layer, 0, pair_rows(i), :] = keys.astype(BF16)
        kvg[layer, 1, pair_rows(i), :] = values.astype(BF16)
        for at in range(DP - 1):
            ag_copy(layer, at).start()

    def head_masks(axis):
        return lax.broadcasted_iota(jnp.int32, (PAIR, PAIR), axis) < HEAD_WIDTH

    first_row, first_lane = head_masks(0), head_masks(1)

    def split_heads(block, mask, axis):
        zero = jnp.zeros_like(block)
        return jnp.concatenate(
            [jnp.where(mask, block, zero), jnp.where(mask, zero, block)], axis=axis
        )

    def own_blocks(both):
        return jnp.where(first_row, both[:, :mem_total], both[:, mem_total:])

    def dot_nt(lhs, rhs):
        return lax.dot_general(lhs, rhs, (((1,), (1,)), ((), ())), preferred_element_type=F32)

    def attend(layer, pair):
        lanes = pair_rows(pair)
        queries, grads = qt_v[layer, lanes, :], gt_v[layer, lanes, :]
        keys, values = kvt[layer, 0, lanes, :], kvt[layer, 1, lanes, :]
        scores = jnp.dot(
            split_heads(keys.T, first_lane, 0), queries, preferred_element_type=F32
        )
        grad_probs = jnp.dot(
            split_heads(values.T, first_lane, 0), grads, preferred_element_type=F32
        )
        probs_b, grad_scores = [], []
        for head in range(2):
            probs_row, grads_row = [], []
            for chunk in range(rows // 128):
                at = (
                    slice(head * mem_total, (head + 1) * mem_total),
                    slice(chunk * 128, (chunk + 1) * 128),
                )
                s, gp = scores[at], grad_probs[at]
                e = jnp.exp(s - jnp.max(s, axis=0, keepdims=True))
                scale = 1.0 / jnp.sum(e, axis=0, keepdims=True)
                delta = jnp.sum(e * gp, axis=0, keepdims=True) * scale
                probs = e * scale
                probs_row.append(probs.astype(BF16))
                grads_row.append((probs * (gp - delta)).astype(BF16))
            probs_b.append(jnp.concatenate(probs_row, axis=1))
            grad_scores.append(jnp.concatenate(grads_row, axis=1))
        probs_b = jnp.concatenate(probs_b, axis=0)
        grad_scores = jnp.concatenate(grad_scores, axis=0)
        att_t[layer, lanes, :] = jnp.dot(
            split_heads(values, first_row, 1), probs_b, preferred_element_type=F32
        ).astype(BF16)
        gq_t[layer, lanes, :] = jnp.dot(
            split_heads(keys, first_row, 1), grad_scores, preferred_element_type=F32
        ).astype(BF16)
        return own_blocks(dot_nt(queries, grad_scores)), own_blocks(dot_nt(grads, probs_b))

    @pl.loop(0, layers)
    def one_layer(layer):
        @pl.when(layer >= 1)
        def _():
            finish_projection(layer)
            reduce(layer - 1)

        far, by_x = attend(layer, i_far), attend(layer, i_x)
        send_part(layer, 0, far[0])
        send_part(layer, 1, far[1])
        send_part(layer, 2, by_x[0])
        hold[0] = by_x[1]
        by_y, mine_both = attend(layer, i_y), attend(layer, i)
        send_part(layer, 3, by_y[1])
        hold[1] = by_y[0]
        for kv in range(2):
            own[layer, kv] = mine_both[kv]
        send_part(layer, 4, hold[0] + came(layer, 1))
        send_part(layer, 5, hold[1] + came(layer, 0))

    def add_memory_gradient(layer):
        for at in range(DP - 1):
            ag_copy(layer, at).wait_recv()
        for kv in range(2):
            term = lax.dot_general(
                kvg[layer, kv],
                w_v[layer, kv, :, mine],
                (((0,), (0,)), ((), ())),
                preferred_element_type=F32,
            ).reshape(CORES, CHIPS, tokens, quarter)
            if layer == 0 and kv == 0:
                gm_v[...] = term
            else:
                gm_v[...] += term

    reduce(layers - 1)

    att_out = pltpu.make_async_copy(att_t, att_hbm, out_sem.at[1])
    gq_out = pltpu.make_async_copy(gq_t, gq_hbm, out_sem.at[2])
    att_out.start()
    gq_out.start()
    for layer in range(layers):
        add_memory_gradient(layer)
    kvg_out = pltpu.make_async_copy(kvg, kvg_hbm, out_sem.at[3])
    kvg_out.start()
    gm_copy = pltpu.make_async_remote_copy(
        src_ref=gm_v.at[1 - core],
        dst_ref=gm_landed,
        send_sem=gm_sem.at[0],
        recv_sem=gm_sem.at[1],
        device_id=sib,
        device_id_type=MESH,
    )
    gm_copy.start()
    for copy in z_copies + d_copies + s_copies:
        copy.wait_send()
    for layer in range(layers):
        for slot in range(6):
            rs_copy(layer, slot).wait_send()
        for at in range(DP - 1):
            ag_copy(layer, at).wait_send()
    gm_copy.wait()
    gm_landed[...] += gm_v[core]
    gm_outs = [
        pltpu.make_async_copy(gm_landed.at[(z + k) % CHIPS], hbm, out_sem.at[4 + k])
        for k, hbm in enumerate((gm0_hbm, gm1_hbm, gm2_hbm, gm3_hbm))
    ]
    for copy in gm_outs:
        copy.start()
    for copy in [mem_out, att_out, gq_out, kvg_out] + gm_outs:
        copy.wait()


def attention(queries, memory, w_key, w_value, grad_out):
    layers, rows, width = queries.shape
    tokens, model = memory.shape
    quarter = model // DP
    mem_total = tokens * CHIPS * CORES
    any_spec = pl.BlockSpec(memory_space=pl.ANY)
    dma = pltpu.SemaphoreType.DMA
    out_shape = (
        jax.ShapeDtypeStruct((layers, width, rows), BF16),
        jax.ShapeDtypeStruct((layers, width, rows), BF16),
        jax.ShapeDtypeStruct((layers, 2, width, mem_total), BF16),
        jax.ShapeDtypeStruct((DP, CORES, CHIPS, tokens, quarter), BF16),
    ) + (jax.ShapeDtypeStruct((tokens, quarter), F32),) * CHIPS
    return pl.pallas_call(
        attention_kernel,
        out_shape=out_shape,
        in_specs=[any_spec, pl.BlockSpec(memory_space=pltpu.HBM)] + [any_spec] * 3,
        out_specs=(any_spec,) * (4 + CHIPS),
        scratch_shapes=[
            pltpu.VMEM(queries.shape, BF16),
            pltpu.VMEM(queries.shape, BF16),
            pltpu.VMEM((layers, width, rows), BF16),
            pltpu.VMEM((layers, width, rows), BF16),
            pltpu.VMEM((layers, width, rows), BF16),
            pltpu.VMEM((layers, width, rows), BF16),
            pltpu.VMEM((layers, 2, width, model), BF16),
            pltpu.VMEM(memory.shape, BF16),
            pltpu.VMEM((DP, CORES, CHIPS, tokens, quarter), BF16),
            pltpu.VMEM((DP, quarter, mem_total), BF16),
            pltpu.VMEM((layers, 2, width, mem_total), F32),
            pltpu.VMEM((layers, 2, width, mem_total), BF16),
            pltpu.VMEM((layers, 6, PAIR, mem_total), BF16),
            pltpu.VMEM((layers, 2, PAIR, mem_total), F32),
            pltpu.VMEM((2, PAIR, mem_total), F32),
            pltpu.VMEM((layers, 6, PAIR, mem_total), BF16),
            pltpu.VMEM((layers, 2, width, mem_total), BF16),
            pltpu.VMEM((CORES, CHIPS, tokens, quarter), F32),
            pltpu.VMEM((CHIPS, tokens, quarter), F32),
            dma((3,)),
            dma((DP, 2)),
            dma((4 + CHIPS,)),
            dma((CHIPS - 1,)),
            dma((CHIPS - 1,)),
            dma((4,)),
            dma((4,)),
            dma((DP,)),
            dma((DP,)),
            dma((layers, 6)),
            dma((layers, 6)),
            dma((layers, DP - 1)),
            dma((layers, DP - 1)),
            dma((2,)),
        ],
        compiler_params=pltpu.CompilerParams(
            collective_id=0, has_side_effects=True, vmem_limit_bytes=60 * 2**20
        ),
        cost_estimate=pl.CostEstimate(
            flops=8 * 10**9, bytes_accessed=35 * 10**6, transcendentals=2 * 10**6
        ),
        name="attention",
    )(queries, memory, w_key, w_value, grad_out)


def weight_kernel(
    kv, kvg_hbm, mem_hbm, turned_hbm, out_hbm, back_hbm,
    kvg_v, mem_v, turned_v, ring, back_v, in_sem, ring_sem, back_sem,
):
    layers, width, _ = kvg_v.shape
    quarter = mem_v.shape[-1]
    slots = ring.shape[0]
    loads = [
        pltpu.make_async_copy(kvg_hbm.at[:, kv], kvg_v, in_sem.at[0]),
        pltpu.make_async_copy(mem_hbm, mem_v, in_sem.at[1]),
        pltpu.make_async_copy(turned_hbm, turned_v, in_sem.at[2]),
    ]
    for copy in loads:
        copy.start()
    loads[0].wait()
    loads[1].wait()

    rows = ring.shape[1]
    blocks = width // rows

    def block_rows(n):
        return pl.ds(pl.multiple_of(n % blocks * rows, rows), rows)

    def write(n):
        return pltpu.make_async_copy(
            ring.at[n % slots],
            out_hbm.at[n // blocks, block_rows(n), :],
            ring_sem.at[n % slots],
        )

    def write_back(layer):
        return pltpu.make_async_copy(back_v.at[layer], back_hbm.at[layer], back_sem.at[layer])

    @pl.loop(0, layers * blocks)
    def step(n):
        layer = n // blocks

        @pl.when(n >= slots)
        def _():
            write(n - slots).wait()

        for j in range(DP):
            ring[n % slots, :, j * quarter : (j + 1) * quarter] = jnp.dot(
                kvg_v[layer, block_rows(n), :], mem_v[j], preferred_element_type=F32
            )
        write(n).start()

        @pl.when(n == 0)
        def _():
            loads[2].wait()

        back_v[layer, :, block_rows(n)] = turned_v[layer, block_rows(n), :].T

        @pl.when(n % blocks == blocks - 1)
        def _():
            write_back(layer).start()

    for n in range(layers * blocks - slots, layers * blocks):
        write(n).wait()
    for layer in range(layers):
        write_back(layer).wait()


def weight_gradient(kvg, mem, turned, kv):
    layers, _, width, mem_total = kvg.shape
    quarter = mem.shape[-1]
    model = DP * quarter
    rows = turned.shape[-1]
    slots = 4
    any_spec = pl.BlockSpec(memory_space=pl.ANY)
    dma = pltpu.SemaphoreType.DMA
    return pl.pallas_call(
        functools.partial(weight_kernel, kv),
        in_specs=[any_spec] * 3,
        out_specs=[any_spec] * 2,
        out_shape=(
            jax.ShapeDtypeStruct((layers, width, model), F32),
            jax.ShapeDtypeStruct((layers, rows, width), BF16),
        ),
        scratch_shapes=[
            pltpu.VMEM((layers, width, mem_total), BF16),
            pltpu.VMEM(mem.shape, BF16),
            pltpu.VMEM(turned.shape, BF16),
            pltpu.VMEM((slots, 2 * PAIR, model), F32),
            pltpu.VMEM((layers, rows, width), BF16),
            dma((3,)),
            dma((slots,)),
            dma((layers,)),
        ],
        compiler_params=pltpu.CompilerParams(vmem_limit_bytes=60 * 2**20),
        cost_estimate=pl.CostEstimate(
            flops=2 * layers * width * mem_total * model,
            bytes_accessed=4 * layers * width * (model + rows),
            transcendentals=0,
        ),
        name=("grad_w_key", "grad_w_value")[kv],
    )(kvg, mem, turned)


def place_kernel(*refs):
    out_ref, sem = refs[-2:]
    quarter = refs[0].shape[-1]
    i = lax.axis_index("dp")
    copies = []
    for k, ref in enumerate(refs[:-2]):
        j = (i + DP - k) % DP
        cols = pl.ds(pl.multiple_of(j * quarter, quarter), quarter)
        copies.append(pltpu.make_async_copy(ref, out_ref.at[:, cols], sem.at[k]))
        copies[-1].start()
    for copy in copies:
        copy.wait()


def fused_shards(queries, memory, w_key, w_value, grad_out):
    attended_t, grad_queries_t, kvg, mem, *gm_parts = attention(
        queries, memory, w_key, w_value, grad_out
    )
    tokens, model = memory.shape
    mem = mem.reshape(DP, tokens * CHIPS * CORES, model // DP)
    gm = gm_parts[0]
    for k in range(1, CHIPS):
        ring = [
            (z * CORES + core, (z + k) % CHIPS * CORES + core)
            for z in range(CHIPS)
            for core in range(CORES)
        ]
        gm = gm + lax.ppermute(gm_parts[k], "mp", ring)
    grad_w_key, attended = weight_gradient(kvg, mem, attended_t, 0)
    grad_w_key, gm = lax.optimization_barrier((grad_w_key, gm))
    quarters = [gm] + [
        lax.ppermute(gm, "dp", [(i, (i + k) % DP) for i in range(DP)]) for k in range(1, DP)
    ]
    grad_w_value, grad_queries = weight_gradient(kvg, mem, grad_queries_t, 1)
    grad_memory = pl.pallas_call(
        place_kernel,
        in_specs=[pl.BlockSpec(memory_space=pl.ANY)] * DP,
        out_specs=pl.BlockSpec(memory_space=pl.ANY),
        out_shape=jax.ShapeDtypeStruct((tokens, model), F32),
        scratch_shapes=[pltpu.SemaphoreType.DMA((DP,))],
        name="place",
    )(*quarters)
    return attended, grad_queries, grad_memory, grad_w_key, grad_w_value


def shards(queries, memory, w_key, w_value, grad_out):
    layers, rows, width = queries.shape
    heads_dev = width // HEAD_WIDTH
    mem_all = lax.all_gather(memory, "mp", axis=0, tiled=True)
    mem_total = mem_all.shape[0]
    keys = jnp.einsum("md,lcd->lmc", mem_all, w_key, preferred_element_type=jnp.float32).astype(
        jnp.bfloat16
    )
    values = jnp.einsum("md,lcd->lmc", mem_all, w_value, preferred_element_type=jnp.float32).astype(
        jnp.bfloat16
    )
    per_head_queries = queries.reshape(layers, rows, heads_dev, HEAD_WIDTH)
    per_head_keys = keys.reshape(layers, mem_total, heads_dev, HEAD_WIDTH)
    per_head_values = values.reshape(layers, mem_total, heads_dev, HEAD_WIDTH)
    head_output_gradient = grad_out.reshape(layers, rows, heads_dev, HEAD_WIDTH)
    attention_logits = jnp.einsum(
        "lrhd,lmhd->lhrm", per_head_queries, per_head_keys, preferred_element_type=jnp.float32
    )
    row_max = jnp.max(attention_logits, axis=-1, keepdims=True)
    exp_scores = jnp.exp(attention_logits - row_max)
    attn_probs = exp_scores / jnp.sum(exp_scores, axis=-1, keepdims=True)
    batch_probabilities = attn_probs.astype(jnp.bfloat16)
    attended = (
        jnp.einsum(
            "lhrm,lmhd->lrhd",
            batch_probabilities,
            per_head_values,
            preferred_element_type=jnp.float32,
        )
        .reshape(layers, rows, width)
        .astype(jnp.bfloat16)
    )
    probability_gradient = jnp.einsum(
        "lrhd,lmhd->lhrm", head_output_gradient, per_head_values, preferred_element_type=jnp.float32
    )
    row_delta = jnp.sum(attn_probs * probability_gradient, axis=-1, keepdims=True)
    logit_gradient = (attn_probs * (probability_gradient - row_delta)).astype(jnp.bfloat16)
    grad_queries = (
        jnp.einsum(
            "lhrm,lmhd->lrhd", logit_gradient, per_head_keys, preferred_element_type=jnp.float32
        )
        .reshape(layers, rows, width)
        .astype(jnp.bfloat16)
    )
    key_part = jnp.einsum(
        "lhrm,lrhd->lmhd", logit_gradient, per_head_queries, preferred_element_type=jnp.float32
    ).reshape(layers, mem_total, width)
    value_part = jnp.einsum(
        "lhrm,lrhd->lmhd",
        batch_probabilities,
        head_output_gradient,
        preferred_element_type=jnp.float32,
    ).reshape(layers, mem_total, width)
    key_sum, value_sum = lax.psum((key_part, value_part), "dp")
    key_gradient = key_sum.astype(jnp.bfloat16)
    value_gradient = value_sum.astype(jnp.bfloat16)
    grad_w_key = jnp.einsum(
        "lmc,md->lcd", key_gradient, mem_all, preferred_element_type=jnp.float32
    )
    grad_w_value = jnp.einsum(
        "lmc,md->lcd", value_gradient, mem_all, preferred_element_type=jnp.float32
    )
    grad_memory = lax.psum_scatter(
        jnp.einsum("lmc,lcd->md", key_gradient, w_key, preferred_element_type=jnp.float32)
        + jnp.einsum("lmc,lcd->md", value_gradient, w_value, preferred_element_type=jnp.float32),
        "mp",
        scatter_dimension=0,
        tiled=True,
    )
    return (attended, grad_queries, grad_memory, grad_w_key, grad_w_value)


def solution(mesh):
    def choose(queries, memory, w_key, w_value, grad_out):
        fits = (
            mesh.shape["dp"] == DP
            and mesh.shape["mp"] == CHIPS * CORES
            and queries.shape[2] == DP * PAIR
            and queries.shape[1] % (128 * DP) == 0
            and memory.shape[0] == PAIR // (CHIPS * CORES)
            and memory.shape[1] % (DP * 128) == 0
        )
        run = fused_shards if fits else shards
        return run(queries, memory, w_key, w_value, grad_out)

    return jax.shard_map(
        choose,
        mesh=mesh,
        in_specs=(
            P(None, "dp", "mp"),
            P("mp", None),
            P(None, "mp", None),
            P(None, "mp", None),
            P(None, "dp", "mp"),
        ),
        out_specs=(
            P(None, "dp", "mp"),
            P(None, "dp", "mp"),
            P("mp", None),
            P(None, "mp", None),
            P(None, "mp", None),
        ),
        check_vma=False,
    )
```

```python
import functools

import jax
import jax.numpy as jnp
from jax import lax
from jax.experimental import pallas as pl
from jax.experimental.pallas import tpu as pltpu
from jax.sharding import PartitionSpec as P

HEAD_WIDTH = 64
PAIR = 2 * HEAD_WIDTH
MESH = pl.DeviceIdType.MESH
F32 = jnp.float32
BF16 = jnp.bfloat16

DP, CHIPS, CORES = 4, 4, 2


def attention_kernel(
    q_hbm, mem_in, wk_hbm, wv_hbm, g_hbm,
    att_hbm, gq_hbm, kvg_hbm, mem_hbm, gm0_hbm, gm1_hbm, gm2_hbm, gm3_hbm,
    q_v, g_v, qt_v, gt_v, att_t, gq_t, w_v, mem_ref, mg, mt, acc, kvt, part, own, hold, landed, kvg,
    gm_v, gm_landed,
    in_sem, w_sem, out_sem, z_send, z_recv, d_send, d_recv, s_send, s_recv,
    rs_send, rs_recv, ag_send, ag_recv, gm_sem,
):
    layers, rows, width = q_v.shape
    tokens = mem_ref.shape[0]
    quarter = mem_ref.shape[1] // DP
    mem_total = tokens * CHIPS * CORES
    i = lax.axis_index("dp")
    me = lax.axis_index("mp")
    z = me // CORES
    core = me % CORES
    sibling = z * CORES + 1 - core

    def z_peer(k):
        return {"dp": i, "mp": ((z + k) % CHIPS) * CORES + core}

    x, y = i % 2, i // 2
    i_x, i_y, i_far = y * 2 + 1 - x, (1 - y) * 2 + x, DP - 1 - i
    order = (i, i_x, i_y, i_far)
    to_x, to_y, to_far = ({"dp": j, "mp": me} for j in (i_x, i_y, i_far))

    sib = {"dp": i, "mp": sibling}

    def columns(step):
        return pl.ds(pl.multiple_of(order[step] * quarter, quarter), quarter)

    def load_w(layer):
        return [
            pltpu.make_async_copy(hbm.at[layer], w_v.at[layer, kv], w_sem.at[layer, kv])
            for kv, hbm in enumerate((wk_hbm, wv_hbm))
        ]

    load_mem = pltpu.make_async_copy(mem_in, mem_ref, in_sem.at[2])
    load_q = pltpu.make_async_copy(q_hbm, q_v, in_sem.at[0])
    load_g = pltpu.make_async_copy(g_hbm, g_v, in_sem.at[1])
    load_mem.start()
    load_q.start()
    load_g.start()
    for layer in range(layers):
        for copy in load_w(layer):
            copy.start()

    barrier = pltpu.get_barrier_semaphore()
    for k in range(1, CHIPS):
        pl.semaphore_signal(barrier, inc=1, device_id=z_peer(k), device_id_type=MESH)
    for peer in (to_x, to_y, to_far, sib):
        pl.semaphore_signal(barrier, inc=1, device_id=peer, device_id_type=MESH)
    load_mem.wait()
    pl.semaphore_wait(barrier, CHIPS - 1 + 4)

    mine = columns(0)
    z_copies = []
    mg[i, core, z] = mem_ref[:, mine]
    for k in range(1, CHIPS):
        z_copies.append(
            pltpu.make_async_remote_copy(
                src_ref=mg.at[i, core, z],
                dst_ref=mg.at[i, core, z],
                send_sem=z_send.at[k - 1],
                recv_sem=z_recv.at[k - 1],
                device_id=z_peer(k),
                device_id_type=MESH,
            )
        )
        z_copies[-1].start()
    for copy in z_copies:
        copy.wait_recv()

    def to_sibling(step):
        block = mg.at[order[step], core]
        return pltpu.make_async_remote_copy(
            src_ref=block,
            dst_ref=block,
            send_sem=s_send.at[step],
            recv_sem=s_recv.at[step],
            device_id=sib,
            device_id_type=MESH,
        )

    def gather_copy(block, at, peer):
        return pltpu.make_async_remote_copy(
            src_ref=block,
            dst_ref=block,
            send_sem=d_send.at[at],
            recv_sem=d_recv.at[at],
            device_id=peer,
            device_id_type=MESH,
        )

    half = CHIPS // 2
    s_copies = [to_sibling(step) for step in range(DP)]
    d_copies = [
        gather_copy(mg.at[i, core], 0, to_x),
        gather_copy(mg.at[i, core], 1, to_y),
        gather_copy(mg.at[i_x, core, pl.ds(0, half)], 2, to_y),
        gather_copy(mg.at[i_y, core, pl.ds(half, half)], 3, to_x),
    ]
    d_copies[0].start()
    d_copies[1].start()
    s_copies[0].start()

    def pair_rows(pair):
        return pl.ds(pl.multiple_of(pair * PAIR, PAIR), PAIR)

    load_q.wait()
    load_g.wait()

    @pl.loop(0, layers * DP)
    def turn(n):
        lanes = pair_rows(n % DP)
        qt_v[n // DP, lanes, :] = q_v[n // DP, :, lanes].T
        gt_v[n // DP, lanes, :] = g_v[n // DP, :, lanes].T

    def project(layer, kv, step):
        return jnp.dot(w_v[layer, kv, :, columns(step)], mt[step], preferred_element_type=F32)

    for step in range(DP):
        if step == 1:
            for near in range(2):
                d_copies[near].wait_recv()
                d_copies[2 + near].start()
                s_copies[1 + near].start()
        elif step == 3:
            d_copies[2].wait_recv()
            d_copies[3].wait_recv()
            s_copies[3].start()
        s_copies[step].wait_recv()
        mt[step] = mg[order[step]].reshape(mem_total, quarter).T
        if step == 0:

            for layer in range(layers):
                for copy in load_w(layer):
                    copy.wait()

                @pl.loop(0, 2)
                def first_quarter(kv):
                    acc[layer, kv] = project(layer, kv, 0)

        elif step < DP - 1:

            @pl.loop(0, 2)
            def layer_0(kv):
                acc[0, kv] += project(0, kv, step)

        else:

            @pl.loop(0, 2)
            def layer_0_last(kv):
                kvt[0, kv] = (acc[0, kv] + project(0, kv, step)).astype(BF16)

    def finish_projection(layer):
        @pl.loop(0, 2)
        def one(kv):
            total = acc[layer, kv]
            for step in range(1, DP):
                total = total + project(layer, kv, step)
            kvt[layer, kv] = total.astype(BF16)

    mem_out = pltpu.make_async_copy(mg, mem_hbm, out_sem.at[0])
    mem_out.start()

    def rs_copy(layer, slot):
        return pltpu.make_async_remote_copy(
            src_ref=part.at[layer, slot],
            dst_ref=landed.at[layer, slot],
            send_sem=rs_send.at[layer, slot],
            recv_sem=rs_recv.at[layer, slot],
            device_id=to_x if slot % 2 == 0 else to_y,
            device_id_type=MESH,
        )

    def send_part(layer, slot, term):
        part[layer, slot] = term.astype(BF16)
        rs_copy(layer, slot).start()

    def came(layer, slot):
        rs_copy(layer, slot).wait_recv()
        return landed[layer, slot].astype(F32)

    def ag_copy(layer, at):
        block = kvg.at[layer, :, pair_rows(i), :]
        return pltpu.make_async_remote_copy(
            src_ref=block,
            dst_ref=block,
            send_sem=ag_send.at[layer, at],
            recv_sem=ag_recv.at[layer, at],
            device_id=(to_far, to_x, to_y)[at],
            device_id_type=MESH,
        )

    def reduce(layer):
        keys = own[layer, 0] + came(layer, 2) + came(layer, 5)
        values = own[layer, 1] + came(layer, 3) + came(layer, 4)
        kvg[layer, 0, pair_rows(i), :] = keys.astype(BF16)
        kvg[layer, 1, pair_rows(i), :] = values.astype(BF16)
        for at in range(DP - 1):
            ag_copy(layer, at).start()

    def head_masks(axis):
        return lax.broadcasted_iota(jnp.int32, (PAIR, PAIR), axis) < HEAD_WIDTH

    first_row, first_lane = head_masks(0), head_masks(1)

    def split_heads(block, mask, axis):
        zero = jnp.zeros_like(block)
        return jnp.concatenate(
            [jnp.where(mask, block, zero), jnp.where(mask, zero, block)], axis=axis
        )

    def own_blocks(both):
        return jnp.where(first_row, both[:, :mem_total], both[:, mem_total:])

    def dot_nt(lhs, rhs):
        return lax.dot_general(lhs, rhs, (((1,), (1,)), ((), ())), preferred_element_type=F32)

    def attend(layer, pair):
        lanes = pair_rows(pair)
        queries, grads = qt_v[layer, lanes, :], gt_v[layer, lanes, :]
        keys, values = kvt[layer, 0, lanes, :], kvt[layer, 1, lanes, :]
        scores = jnp.dot(
            split_heads(keys.T, first_lane, 0), queries, preferred_element_type=F32
        )
        grad_probs = jnp.dot(
            split_heads(values.T, first_lane, 0), grads, preferred_element_type=F32
        )
        probs_b, grad_scores = [], []
        for head in range(2):
            probs_row, grads_row = [], []
            for chunk in range(rows // 128):
                at = (
                    slice(head * mem_total, (head + 1) * mem_total),
                    slice(chunk * 128, (chunk + 1) * 128),
                )
                s, gp = scores[at], grad_probs[at]
                e = jnp.exp(s - jnp.max(s, axis=0, keepdims=True))
                scale = 1.0 / jnp.sum(e, axis=0, keepdims=True)
                delta = jnp.sum(e * gp, axis=0, keepdims=True) * scale
                probs = e * scale
                probs_row.append(probs.astype(BF16))
                grads_row.append((probs * (gp - delta)).astype(BF16))
            probs_b.append(jnp.concatenate(probs_row, axis=1))
            grad_scores.append(jnp.concatenate(grads_row, axis=1))
        probs_b = jnp.concatenate(probs_b, axis=0)
        grad_scores = jnp.concatenate(grad_scores, axis=0)
        att_t[layer, lanes, :] = jnp.dot(
            split_heads(values, first_row, 1), probs_b, preferred_element_type=F32
        ).astype(BF16)
        gq_t[layer, lanes, :] = jnp.dot(
            split_heads(keys, first_row, 1), grad_scores, preferred_element_type=F32
        ).astype(BF16)
        return own_blocks(dot_nt(queries, grad_scores)), own_blocks(dot_nt(grads, probs_b))

    @pl.loop(0, layers)
    def one_layer(layer):
        @pl.when(layer >= 1)
        def _():
            finish_projection(layer)
            reduce(layer - 1)

        far, by_x = attend(layer, i_far), attend(layer, i_x)
        send_part(layer, 0, far[0])
        send_part(layer, 1, far[1])
        send_part(layer, 2, by_x[0])
        hold[0] = by_x[1]
        by_y, mine_both = attend(layer, i_y), attend(layer, i)
        send_part(layer, 3, by_y[1])
        hold[1] = by_y[0]
        for kv in range(2):
            own[layer, kv] = mine_both[kv]
        send_part(layer, 4, hold[0] + came(layer, 1))
        send_part(layer, 5, hold[1] + came(layer, 0))

    def add_memory_gradient(layer):
        for at in range(DP - 1):
            ag_copy(layer, at).wait_recv()
        for kv in range(2):
            term = lax.dot_general(
                kvg[layer, kv],
                w_v[layer, kv, :, mine],
                (((0,), (0,)), ((), ())),
                preferred_element_type=F32,
            ).reshape(CORES, CHIPS, tokens, quarter)
            if layer == 0 and kv == 0:
                gm_v[...] = term
            else:
                gm_v[...] += term

    reduce(layers - 1)

    att_out = pltpu.make_async_copy(att_t, att_hbm, out_sem.at[1])
    gq_out = pltpu.make_async_copy(gq_t, gq_hbm, out_sem.at[2])
    att_out.start()
    gq_out.start()
    for layer in range(layers):
        add_memory_gradient(layer)
    kvg_out = pltpu.make_async_copy(kvg, kvg_hbm, out_sem.at[3])
    kvg_out.start()
    gm_copy = pltpu.make_async_remote_copy(
        src_ref=gm_v.at[1 - core],
        dst_ref=gm_landed,
        send_sem=gm_sem.at[0],
        recv_sem=gm_sem.at[1],
        device_id=sib,
        device_id_type=MESH,
    )
    gm_copy.start()
    for copy in z_copies + d_copies + s_copies:
        copy.wait_send()
    for layer in range(layers):
        for slot in range(6):
            rs_copy(layer, slot).wait_send()
        for at in range(DP - 1):
            ag_copy(layer, at).wait_send()
    gm_copy.wait()
    gm_landed[...] += gm_v[core]
    gm_outs = [
        pltpu.make_async_copy(gm_landed.at[(z + k) % CHIPS], hbm, out_sem.at[4 + k])
        for k, hbm in enumerate((gm0_hbm, gm1_hbm, gm2_hbm, gm3_hbm))
    ]
    for copy in gm_outs:
        copy.start()
    for copy in [mem_out, att_out, gq_out, kvg_out] + gm_outs:
        copy.wait()


def attention(queries, memory, w_key, w_value, grad_out):
    layers, rows, width = queries.shape
    tokens, model = memory.shape
    quarter = model // DP
    mem_total = tokens * CHIPS * CORES
    any_spec = pl.BlockSpec(memory_space=pl.ANY)
    dma = pltpu.SemaphoreType.DMA
    out_shape = (
        jax.ShapeDtypeStruct((layers, width, rows), BF16),
        jax.ShapeDtypeStruct((layers, width, rows), BF16),
        jax.ShapeDtypeStruct((layers, 2, width, mem_total), BF16),
        jax.ShapeDtypeStruct((DP, CORES, CHIPS, tokens, quarter), BF16),
    ) + (jax.ShapeDtypeStruct((tokens, quarter), F32),) * CHIPS
    return pl.pallas_call(
        attention_kernel,
        out_shape=out_shape,
        in_specs=[any_spec, pl.BlockSpec(memory_space=pltpu.HBM)] + [any_spec] * 3,
        out_specs=(any_spec,) * (4 + CHIPS),
        scratch_shapes=[
            pltpu.VMEM(queries.shape, BF16),
            pltpu.VMEM(queries.shape, BF16),
            pltpu.VMEM((layers, width, rows), BF16),
            pltpu.VMEM((layers, width, rows), BF16),
            pltpu.VMEM((layers, width, rows), BF16),
            pltpu.VMEM((layers, width, rows), BF16),
            pltpu.VMEM((layers, 2, width, model), BF16),
            pltpu.VMEM(memory.shape, BF16),
            pltpu.VMEM((DP, CORES, CHIPS, tokens, quarter), BF16),
            pltpu.VMEM((DP, quarter, mem_total), BF16),
            pltpu.VMEM((layers, 2, width, mem_total), F32),
            pltpu.VMEM((layers, 2, width, mem_total), BF16),
            pltpu.VMEM((layers, 6, PAIR, mem_total), BF16),
            pltpu.VMEM((layers, 2, PAIR, mem_total), F32),
            pltpu.VMEM((2, PAIR, mem_total), F32),
            pltpu.VMEM((layers, 6, PAIR, mem_total), BF16),
            pltpu.VMEM((layers, 2, width, mem_total), BF16),
            pltpu.VMEM((CORES, CHIPS, tokens, quarter), F32),
            pltpu.VMEM((CHIPS, tokens, quarter), F32),
            dma((3,)),
            dma((layers, 2)),
            dma((4 + CHIPS,)),
            dma((CHIPS - 1,)),
            dma((CHIPS - 1,)),
            dma((4,)),
            dma((4,)),
            dma((DP,)),
            dma((DP,)),
            dma((layers, 6)),
            dma((layers, 6)),
            dma((layers, DP - 1)),
            dma((layers, DP - 1)),
            dma((2,)),
        ],
        compiler_params=pltpu.CompilerParams(
            collective_id=0, has_side_effects=True, vmem_limit_bytes=60 * 2**20
        ),
        cost_estimate=pl.CostEstimate(
            flops=8 * 10**9, bytes_accessed=35 * 10**6, transcendentals=2 * 10**6
        ),
        name="attention",
    )(queries, memory, w_key, w_value, grad_out)


def weight_kernel(
    kv, kvg_hbm, mem_hbm, turned_hbm, out_hbm, back_hbm,
    kvg_v, mem_v, turned_v, ring, back_v, in_sem, ring_sem, back_sem,
):
    layers, width, _ = kvg_v.shape
    quarter = mem_v.shape[-1]
    slots = ring.shape[0]
    loads = [
        pltpu.make_async_copy(kvg_hbm.at[:, kv], kvg_v, in_sem.at[0]),
        pltpu.make_async_copy(mem_hbm, mem_v, in_sem.at[1]),
        pltpu.make_async_copy(turned_hbm, turned_v, in_sem.at[2]),
    ]
    for copy in loads:
        copy.start()
    loads[0].wait()
    loads[1].wait()

    rows = ring.shape[1]
    blocks = width // rows

    def block_rows(n):
        return pl.ds(pl.multiple_of(n % blocks * rows, rows), rows)

    def write(n):
        return pltpu.make_async_copy(
            ring.at[n % slots],
            out_hbm.at[n // blocks, block_rows(n), :],
            ring_sem.at[n % slots],
        )

    def write_back(layer):
        return pltpu.make_async_copy(back_v.at[layer], back_hbm.at[layer], back_sem.at[layer])

    @pl.loop(0, layers * blocks)
    def step(n):
        layer = n // blocks

        @pl.when(n >= slots)
        def _():
            write(n - slots).wait()

        for j in range(DP):
            ring[n % slots, :, j * quarter : (j + 1) * quarter] = jnp.dot(
                kvg_v[layer, block_rows(n), :], mem_v[j], preferred_element_type=F32
            )
        write(n).start()

        @pl.when(n == 0)
        def _():
            loads[2].wait()

        back_v[layer, :, block_rows(n)] = turned_v[layer, block_rows(n), :].T

        @pl.when(n % blocks == blocks - 1)
        def _():
            write_back(layer).start()

    for n in range(layers * blocks - slots, layers * blocks):
        write(n).wait()
    for layer in range(layers):
        write_back(layer).wait()


def weight_gradient(kvg, mem, turned, kv):
    layers, _, width, mem_total = kvg.shape
    quarter = mem.shape[-1]
    model = DP * quarter
    rows = turned.shape[-1]
    slots = 4
    any_spec = pl.BlockSpec(memory_space=pl.ANY)
    dma = pltpu.SemaphoreType.DMA
    return pl.pallas_call(
        functools.partial(weight_kernel, kv),
        in_specs=[any_spec] * 3,
        out_specs=[any_spec] * 2,
        out_shape=(
            jax.ShapeDtypeStruct((layers, width, model), F32),
            jax.ShapeDtypeStruct((layers, rows, width), BF16),
        ),
        scratch_shapes=[
            pltpu.VMEM((layers, width, mem_total), BF16),
            pltpu.VMEM(mem.shape, BF16),
            pltpu.VMEM(turned.shape, BF16),
            pltpu.VMEM((slots, PAIR, model), F32),
            pltpu.VMEM((layers, rows, width), BF16),
            dma((3,)),
            dma((slots,)),
            dma((layers,)),
        ],
        compiler_params=pltpu.CompilerParams(vmem_limit_bytes=60 * 2**20),
        cost_estimate=pl.CostEstimate(
            flops=2 * layers * width * mem_total * model,
            bytes_accessed=4 * layers * width * (model + rows),
            transcendentals=0,
        ),
        name=("grad_w_key", "grad_w_value")[kv],
    )(kvg, mem, turned)


def place_kernel(*refs):
    out_ref = refs[-1]
    quarter = refs[0].shape[-1]
    i = lax.axis_index("dp")
    for k, ref in enumerate(refs[:-1]):
        j = (i + DP - k) % DP
        out_ref[:, pl.ds(pl.multiple_of(j * quarter, quarter), quarter)] = ref[...]


def fused_shards(queries, memory, w_key, w_value, grad_out):
    attended_t, grad_queries_t, kvg, mem, *gm_parts = attention(
        queries, memory, w_key, w_value, grad_out
    )
    tokens, model = memory.shape
    mem = mem.reshape(DP, tokens * CHIPS * CORES, model // DP)
    gm = gm_parts[0]
    for k in range(1, CHIPS):
        ring = [
            (z * CORES + core, (z + k) % CHIPS * CORES + core)
            for z in range(CHIPS)
            for core in range(CORES)
        ]
        gm = gm + lax.ppermute(gm_parts[k], "mp", ring)
    grad_w_key, attended = weight_gradient(kvg, mem, attended_t, 0)
    grad_w_key, gm = lax.optimization_barrier((grad_w_key, gm))
    quarters = [gm] + [
        lax.ppermute(gm, "dp", [(i, (i + k) % DP) for i in range(DP)]) for k in range(1, DP)
    ]
    grad_w_value, grad_queries = weight_gradient(kvg, mem, grad_queries_t, 1)
    grad_memory = pl.pallas_call(
        place_kernel,
        in_specs=[pl.BlockSpec(memory_space=pltpu.VMEM)] * DP,
        out_specs=pl.BlockSpec(memory_space=pltpu.VMEM),
        out_shape=jax.ShapeDtypeStruct((tokens, model), F32),
        name="place",
    )(*quarters)
    return attended, grad_queries, grad_memory, grad_w_key, grad_w_value


def shards(queries, memory, w_key, w_value, grad_out):
    layers, rows, width = queries.shape
    heads_dev = width // HEAD_WIDTH
    mem_all = lax.all_gather(memory, "mp", axis=0, tiled=True)
    mem_total = mem_all.shape[0]
    keys = jnp.einsum("md,lcd->lmc", mem_all, w_key, preferred_element_type=jnp.float32).astype(
        jnp.bfloat16
    )
    values = jnp.einsum("md,lcd->lmc", mem_all, w_value, preferred_element_type=jnp.float32).astype(
        jnp.bfloat16
    )
    per_head_queries = queries.reshape(layers, rows, heads_dev, HEAD_WIDTH)
    per_head_keys = keys.reshape(layers, mem_total, heads_dev, HEAD_WIDTH)
    per_head_values = values.reshape(layers, mem_total, heads_dev, HEAD_WIDTH)
    head_output_gradient = grad_out.reshape(layers, rows, heads_dev, HEAD_WIDTH)
    attention_logits = jnp.einsum(
        "lrhd,lmhd->lhrm", per_head_queries, per_head_keys, preferred_element_type=jnp.float32
    )
    row_max = jnp.max(attention_logits, axis=-1, keepdims=True)
    exp_scores = jnp.exp(attention_logits - row_max)
    attn_probs = exp_scores / jnp.sum(exp_scores, axis=-1, keepdims=True)
    batch_probabilities = attn_probs.astype(jnp.bfloat16)
    attended = (
        jnp.einsum(
            "lhrm,lmhd->lrhd",
            batch_probabilities,
            per_head_values,
            preferred_element_type=jnp.float32,
        )
        .reshape(layers, rows, width)
        .astype(jnp.bfloat16)
    )
    probability_gradient = jnp.einsum(
        "lrhd,lmhd->lhrm", head_output_gradient, per_head_values, preferred_element_type=jnp.float32
    )
    row_delta = jnp.sum(attn_probs * probability_gradient, axis=-1, keepdims=True)
    logit_gradient = (attn_probs * (probability_gradient - row_delta)).astype(jnp.bfloat16)
    grad_queries = (
        jnp.einsum(
            "lhrm,lmhd->lrhd", logit_gradient, per_head_keys, preferred_element_type=jnp.float32
        )
        .reshape(layers, rows, width)
        .astype(jnp.bfloat16)
    )
    key_part = jnp.einsum(
        "lhrm,lrhd->lmhd", logit_gradient, per_head_queries, preferred_element_type=jnp.float32
    ).reshape(layers, mem_total, width)
    value_part = jnp.einsum(
        "lhrm,lrhd->lmhd",
        batch_probabilities,
        head_output_gradient,
        preferred_element_type=jnp.float32,
    ).reshape(layers, mem_total, width)
    key_sum, value_sum = lax.psum((key_part, value_part), "dp")
    key_gradient = key_sum.astype(jnp.bfloat16)
    value_gradient = value_sum.astype(jnp.bfloat16)
    grad_w_key = jnp.einsum(
        "lmc,md->lcd", key_gradient, mem_all, preferred_element_type=jnp.float32
    )
    grad_w_value = jnp.einsum(
        "lmc,md->lcd", value_gradient, mem_all, preferred_element_type=jnp.float32
    )
    grad_memory = lax.psum_scatter(
        jnp.einsum("lmc,lcd->md", key_gradient, w_key, preferred_element_type=jnp.float32)
        + jnp.einsum("lmc,lcd->md", value_gradient, w_value, preferred_element_type=jnp.float32),
        "mp",
        scatter_dimension=0,
        tiled=True,
    )
    return (attended, grad_queries, grad_memory, grad_w_key, grad_w_value)


def solution(mesh):
    def choose(queries, memory, w_key, w_value, grad_out):
        fits = (
            mesh.shape["dp"] == DP
            and mesh.shape["mp"] == CHIPS * CORES
            and queries.shape[2] == DP * PAIR
            and queries.shape[1] % (128 * DP) == 0
            and memory.shape[0] == PAIR // (CHIPS * CORES)
            and memory.shape[1] % (DP * 128) == 0
        )
        run = fused_shards if fits else shards
        return run(queries, memory, w_key, w_value, grad_out)

    return jax.shard_map(
        choose,
        mesh=mesh,
        in_specs=(
            P(None, "dp", "mp"),
            P("mp", None),
            P(None, "mp", None),
            P(None, "mp", None),
            P(None, "dp", "mp"),
        ),
        out_specs=(
            P(None, "dp", "mp"),
            P(None, "dp", "mp"),
            P("mp", None),
            P(None, "mp", None),
            P(None, "mp", None),
        ),
        check_vma=False,
    )
```
